256 devices in a mesh: gx: 16 (over y, x_hi, core), gy: 16 (over x_lo, z).
Axes of the slice: x: 4 (x_hi: 2, x_lo: 2; x = x_hi * 2 + x_lo), y: 4, z: 8, core: 2. Of those that a mesh axis runs over, the one named last changes fastest.
Arguments:
- cost: float32 [16, 2048, 2048], P(None, 'gx', 'gy'), may hold values from 0 to 7.5
- density_start: float32 [16, 2048, 2048], P(None, 'gx', 'gy'), may hold values from 0.125 to 4.5
- coupling: float32 [16, 16], replicated, may hold values from 0 to 0.25
Outputs:
- value: float32 [16, 2048, 2048], P(None, 'gx', 'gy')
- density: float32 [16, 2048, 2048], P(None, 'gx', 'gy')
- ergodic: float32 [16], replicated
The draws below stay inside these ranges and needn't reach their ends.
All inputs are finite; a program needn't handle non-finite values.
Results may differ from the reference program's by a relative error of at most 0.0003.
Values sent between devices are 32-bit elements; how exact they have to be, the bound alone decides.
No kernel may reach another device: no remote copies, remote signals or barrier semaphores. Data moves between devices by JAX's collectives and lax.ppermute only.
A program may use at most 64 MiB of HBM per device.

```python
import jax
import jax.numpy as jnp
from jax import lax

K = 16
PICARD = 1
SWEEPS = 5
NX = 2048
NY = 2048


def draw_cost(key, part):
    rows = jnp.arange(NX, dtype=jnp.float32) / NX
    cols = jnp.arange(NY, dtype=jnp.float32) / NY
    ramp = 0.5 + rows[:, None] + cols[None, :]
    base = jax.random.uniform(key, (K, NX, NY), jnp.float32, 0.0, 2.0)
    return base * ramp[None]


def draw_density_start(key, part):
    rows = jnp.arange(NX, dtype=jnp.float32) / NX
    cols = jnp.arange(NY, dtype=jnp.float32) / NY
    ramp = (0.5 + rows[:, None]) * (0.5 + cols[None, :])
    base = jax.random.uniform(key, (K, NX, NY), jnp.float32, 0.5, 2.0)
    return base * ramp[None]


def setup_inputs(seed: int = 0) -> dict:
    arg_keys = jax.random.split(jax.random.key(seed), 4)
    cost = draw_cost(jax.random.fold_in(arg_keys[3], 71), 0)
    density_start = draw_density_start(jax.random.fold_in(arg_keys[3], 71), 0)
    coupling = jnp.clip(jax.random.uniform(arg_keys[2], (K, K), jnp.float32, 0.0, 0.25), 0.0, 0.25)
    return dict(cost=cost, density_start=density_start, coupling=coupling)


viscosity = 0.5
theta = 2.0


def rates(u):
    u_xp = jnp.roll(u, -1, axis=0)
    u_xm = jnp.roll(u, 1, axis=0)
    u_yp = jnp.roll(u, -1, axis=1)
    u_ym = jnp.roll(u, 1, axis=1)
    vx = -(u_xp - u_xm) * 0.5
    vy = -(u_yp - u_ym) * 0.5
    r_xp = viscosity + jnp.maximum(vx, 0.0)
    r_xm = viscosity + jnp.maximum(-vx, 0.0)
    r_yp = viscosity + jnp.maximum(vy, 0.0)
    r_ym = viscosity + jnp.maximum(-vy, 0.0)
    total = r_xp + r_xm + r_yp + r_ym
    speed = (vx * vx + vy * vy) * 0.5
    return (r_xp, r_xm, r_yp, r_ym), (u_xp, u_xm, u_yp, u_ym), total, speed


def one_class(items):
    source, value, density, lam = items
    for sweep in range(SWEEPS):
        (r_xp, r_xm, r_yp, r_ym), (u_xp, u_xm, u_yp, u_ym), total, speed = rates(value)
        trial = (source + speed - lam + r_xp * u_xp + r_xm * u_xm + r_yp * u_yp + r_ym * u_ym) / total
        shift = jnp.mean(trial)
        lam = lam + theta * shift
        value = trial - shift
    (r_xp, r_xm, r_yp, r_ym), unused, total, speed = rates(value)
    c_xp = jnp.roll(r_xm, -1, axis=0) / total
    c_xm = jnp.roll(r_xp, 1, axis=0) / total
    c_yp = jnp.roll(r_ym, -1, axis=1) / total
    c_ym = jnp.roll(r_yp, 1, axis=1) / total
    for sweep in range(SWEEPS):
        fresh = (c_xp * jnp.roll(density, -1, axis=0) + c_xm * jnp.roll(density, 1, axis=0)
                 + c_yp * jnp.roll(density, -1, axis=1) + c_ym * jnp.roll(density, 1, axis=1))
        density = fresh / jnp.mean(fresh)
    return value, density, lam


def reference(cost, density_start, coupling):
    value = jnp.zeros(cost.shape, jnp.float32)
    density = density_start
    ergodic = jnp.zeros((cost.shape[0],), jnp.float32)
    for picard in range(PICARD):
        source = cost + jnp.einsum("kj,jxy->kxy", coupling, density, precision=lax.Precision.HIGHEST)
        value, density, ergodic = lax.map(one_class, (source, value, density, ergodic))
    return value, density, ergodic
```

```python
import functools

import jax
import jax.numpy as jnp
from jax import lax
from jax.experimental import pallas as pl
from jax.experimental.pallas import tpu as pltpu
from jax.sharding import Mesh
from jax.sharding import PartitionSpec as P

HALO = 10
D_HALO = 5
PAD = 2
ROW0 = PAD + HALO
N = 128
ROWS = N + 2 * ROW0
K = 16
SUB = 24
AXES = ("y", "xh", "c", "xl", "z")
GX = ("y", "xh", "c")
GY = ("xl", "z")
DEVICES = 256
CELLS = 2048.0 * 2048.0
SLOT = (0, 16, 64, 80)
BLOCK = 4
F32 = jnp.float32


def lanes(shape):
    return lax.broadcasted_iota(jnp.int32, shape, 1)


def roll(x, shift):
    return pltpu.roll(x, shift % 128, 1)


def between(lane, low, high):
    return (lane >= low) & (lane < high)


def recip(x):
    r = pl.reciprocal(x, approx=True)
    return r * (2.0 - x * r)


def pack(rows, left):
    lane = lanes((8, 128))
    out = jnp.zeros((8, 128), F32)
    for (s0, s1, d0, d1), base in zip(rows, SLOT):
        for half, (s, d) in enumerate(((s0, d0), (s1, d1))):
            at = base + 32 * half
            ds = roll(s, at if left else at + HALO)
            dd = roll(d, at + HALO if left else at + HALO + D_HALO)
            out = jnp.where(between(lane, at, at + HALO), ds, out)
            out = jnp.where(between(lane, at + HALO, at + HALO + D_HALO), dd, out)
    return out


def windows(a, b):
    lane = lanes((8, 128))
    left = jnp.where(lane < 32, roll(a, 10), roll(b, 42))
    right = jnp.where(lane < 96, roll(a, 86), roll(b, 118))
    return jnp.where(lane < 64, left, right)


def halo_masks():
    lane = lanes((8, 128))
    left = between(lane, 0, 10) | between(lane, 32, 42)
    right = between(lane, 86, 96) | between(lane, 118, 128)
    return left, right


def beyond(window, from_left, from_right, i, masks, density):
    base = SLOT[i]
    a = roll(from_left, -base - 5 if density else -base)
    b = roll(from_right, 76 - base if density else 86 - base)
    return jnp.where(masks[0], a, jnp.where(masks[1], b, window))


def own(total, margin):
    lane = lanes((K, 128))
    main = jnp.where(between(lane, margin, N - margin), total[:K], 0.0)
    main = jnp.sum(main, axis=1, keepdims=True)
    if margin == 0:
        return main
    edge = total[K:]
    lane = lanes((8, 128))
    halves = []
    for half in range(2):
        at = 32 * half
        mask = between(lane, at + 10, at + 10 + margin) | between(lane, 64 + at + 22 - margin, 64 + at + 22)
        halves.append(jnp.sum(jnp.where(mask, edge, 0.0), axis=1, keepdims=True))
    return main + jnp.concatenate(halves, axis=0)


def to_row(columns):
    lane, cls = lanes((K, 128)), lax.broadcasted_iota(jnp.int32, (K, 128), 0)
    grid = jnp.zeros((K, 128), F32)
    for i, column in enumerate(columns):
        grid = jnp.where(lane == cls + K * i, column, grid)
    return jnp.sum(grid, axis=0, keepdims=True)


def from_row(row, i):
    lane, cls = lanes((K, 128)), lax.broadcasted_iota(jnp.int32, (K, 128), 0)
    return jnp.sum(jnp.where(lane == cls + K * i, row, 0.0), axis=1, keepdims=True)


def spread(column):
    wide = jnp.broadcast_to(column, (K, 128))
    lane = lanes((8, 128))
    edge = jnp.where((lane // 32) % 2 == 0, wide[:8], wide[8:])
    return jnp.concatenate([wide, edge], axis=0)


def parts(up, mid, down, s):
    left, right = roll(mid, 1), roll(mid, -1)
    px = 2.0 + jnp.abs(up - down)
    py = 2.0 + jnp.abs(left - right)
    n = s + (px * (2.0 * (up + down) + (4.0 - px)) + py * (2.0 * (left + right) + (4.0 - py)))
    return n, recip(px + py)


def row_loop(first, count, body, init=0):
    blocks = -(-count // BLOCK)
    first = first - (blocks * BLOCK - count) // 2

    def step(i, carry):
        return body(first + i * BLOCK, carry)

    return lax.fori_loop(0, blocks, step, init)


def sweep(src, s_ref, dst, lam8, minus, margin, summed=False):
    def body(r, total):
        rows = [src[r - 1 + i] for i in range(BLOCK + 2)]
        for i in range(BLOCK):
            n, inv = parts(rows[i], rows[i + 1], rows[i + 2], s_ref[r + i] - lam8)
            w = n * (0.25 * inv)
            if minus is not None:
                w = w - minus
            dst[r + i] = w
        return total

    row_loop(PAD + margin, ROWS - 2 * (PAD + margin), body)
    if summed:
        def add(r, total):
            for i in range(BLOCK):
                total = total + dst[r + i]
            return total

        return row_loop(ROW0, N, add, jnp.zeros((SUB, 128), F32))


def sweep_sums(src, s_ref, half):
    def body(r, carry):
        a, b = carry
        rows = [src[r - 1 + i] for i in range(BLOCK + 2)]
        if half:
            rows = [row * 0.0625 + 0.5 for row in rows]
        for i in range(BLOCK):
            n, inv = parts(rows[i], rows[i + 1], rows[i + 2], s_ref[r + i])
            a = a + n * inv
            b = b + inv
        return a, b

    zero = jnp.zeros((SUB, 128), F32)
    return row_loop(ROW0, N, body, (zero, zero))


def source_kernel(c_ref, cost_ref, d_ref, sx, dx, top, bottom, to_left, to_right):
    s2, d2 = sx.reshape(ROWS * SUB, 128), dx.reshape(ROWS * SUB, 128)

    def chunk(i, carry):
        r = pl.multiple_of(i * 8, 8)
        dens = [d_ref[j, pl.ds(r, 8), :] for j in range(K)]
        base = (ROW0 + r) * SUB
        for j in range(K):
            d2[pl.ds(base + j, 8, stride=SUB), :] = dens[j]
        for k in range(K):
            acc = cost_ref[k, pl.ds(r, 8), :]
            for j in range(K):
                acc = acc + c_ref[k, j] * dens[j]
            s2[pl.ds(base + k, 8, stride=SUB), :] = acc * 8.0 - 8.0
        return carry

    lax.fori_loop(0, N // 8, chunk, 0)

    def group(g, carry):
        r = ROW0 + g * 4
        rows = [(sx[r + i, 0:8], sx[r + i, 8:16], dx[r + i, 0:8], dx[r + i, 8:16]) for i in range(4)]
        to_left[g] = pack(rows, True)
        to_right[g] = pack(rows, False)
        return carry

    lax.fori_loop(0, N // 4, group, 0)
    for i in range(HALO):
        top[i] = sx[ROW0 + i, 0:K]
        bottom[i] = sx[ROW0 + N - HALO + i, 0:K]
    for i in range(D_HALO):
        top[HALO + i] = dx[ROW0 + i, 0:K]
        bottom[HALO + i] = dx[ROW0 + N - D_HALO + i, 0:K]


def halo_rows():
    return [(i, PAD + i) for i in range(HALO)] + [(HALO + i, ROW0 + N + i) for i in range(HALO)]


def first_sums_kernel(s_in, d_in, above, below, from_left, from_right, sx, dx, to_left, to_right, sums):
    del s_in, d_in
    for i in range(HALO):
        sx[PAD + i, 0:K] = above[i]
        sx[ROW0 + N + i, 0:K] = below[i]
    for i in range(D_HALO):
        dx[ROW0 - D_HALO + i, 0:K] = above[HALO + i]
        dx[ROW0 + N + i, 0:K] = below[HALO + i]
    zero = jnp.zeros((8, 128), F32)
    tiles = []
    for i in range(HALO):
        d = above[HALO + i - (HALO - D_HALO)] if i >= HALO - D_HALO else None
        tiles.append((above[i], d, PAD + i))
    for i in range(HALO):
        d = below[HALO + i] if i < D_HALO else None
        tiles.append((below[i], d, ROW0 + N + i))
    packed = []
    for s, d, at in tiles:
        sx[at, K:SUB] = windows(s[:8], s[8:])
        if d is not None:
            dx[at, K:SUB] = windows(d[:8], d[8:])
            packed.append((s[:8], s[8:], d[:8], d[8:]))
        else:
            packed.append((s[:8], s[8:], zero, zero))
    for g in range(5):
        to_left[g] = pack(packed[4 * g : 4 * g + 4], True)
        to_right[g] = pack(packed[4 * g : 4 * g + 4], False)

    masks = halo_masks()

    def group(g, total):
        r = ROW0 + g * 4
        fl, fr = from_left[g], from_right[g]
        for i in range(4):
            s = sx[r + i, 0:K]
            total = total + s
            sx[r + i, K:SUB] = beyond(windows(s[:8], s[8:]), fl, fr, i, masks, False)
            d = dx[r + i, 0:K]
            dx[r + i, K:SUB] = beyond(windows(d[:8], d[8:]), fl, fr, i, masks, True)
        return total

    total = lax.fori_loop(0, N // 4, group, jnp.zeros((K, 128), F32))
    a, b = sweep_sums(sx, sx, True)
    sums[...] = to_row([jnp.sum(total, axis=1, keepdims=True), own(a, 1), own(b, 1)])


def first_means(row):
    lam1 = from_row(row, 0) * (0.125 / CELLS) + 1.0
    mean2 = from_row(row, 1) * (0.25 / CELLS) - lam1 * (from_row(row, 2) * (2.0 / CELLS))
    return lam1, 2.0 * mean2, mean2


def second_means(row, lam2):
    lam3 = lam2 + from_row(row, 0) * (2.0 / CELLS)
    mean4 = from_row(row, 1) * (0.25 / CELLS) - lam3 * (from_row(row, 2) * (2.0 / CELLS))
    return lam3, lam2 + 2.0 * mean4, mean4


def second_sums_kernel(s_in, d_in, from_left, from_right, row1, sx, dx, w3, sums, w1, v2):
    del s_in, d_in
    masks = halo_masks()
    for i, at in halo_rows():
        fl, fr = from_left[i // 4], from_right[i // 4]
        sx[at, K:SUB] = beyond(sx[at, K:SUB], fl, fr, i % 4, masks, False)
        if HALO - D_HALO <= i < HALO + D_HALO:
            dx[at, K:SUB] = beyond(dx[at, K:SUB], fl, fr, i % 4, masks, True)

    def start(r, carry):
        for i in range(BLOCK):
            w1[r + i] = sx[r + i] * 0.0625 + 0.5
        return carry

    row_loop(PAD, ROWS - 2 * PAD, start)
    lam1, lam2, mean2 = first_means(row1[...])
    sweep(w1, sx, v2, spread(8.0 * lam1), spread(mean2), 1)
    total = sweep(v2, sx, w3, spread(8.0 * lam2), None, 2, True)
    a, b = sweep_sums(w3, sx, False)
    sums[...] = to_row([own(total, 2), own(a, 3), own(b, 3)])


def transpose_out(src, scratch, out):
    lane = lanes((8, 128))
    low, high = lane < 10, lane >= 118

    def body(g, carry):
        for i in range(4):
            r = g * 4 + i
            e = src[ROW0 + r, K:SUB]
            for half in range(2):
                a = src[ROW0 + r, 8 * half : 8 * half + 8]
                left = roll(e, -10 - 32 * half)
                right = roll(e, 42 - 32 * half)
                scratch[r, 8 * half : 8 * half + 8] = jnp.where(low, left, jnp.where(high, right, a))
        return carry

    lax.fori_loop(0, N // 4, body, 0)
    flat = scratch.reshape(N * K, 128)

    def chunk(i, carry):
        r = pl.multiple_of(i * 8, 8)
        for k in range(K):
            out[k, pl.ds(r, 8), :] = flat[pl.ds(r * K + k, 8, stride=K), :]
        return carry

    lax.fori_loop(0, N // 8, chunk, 0)


def last_sums_kernel(sx, dx, w3, row1, row2, value, density, sums, v4, w5, cs, da, db, scratch):
    _, lam2, _ = first_means(row1[...])
    lam3, lam4, mean4 = second_means(row2[...], lam2)
    sweep(w3, sx, v4, spread(8.0 * lam3), spread(mean4), 3)
    total5 = sweep(v4, sx, w5, spread(8.0 * lam4), None, 4, True)

    def weigh(r, carry):
        rows = [w5[r - 2 + i] for i in range(BLOCK + 4)]
        for i in range(BLOCK):
            u = rows[i + 2]
            t = 4.0 + jnp.abs(rows[i + 1] - rows[i + 3]) + jnp.abs(roll(u, 1) - roll(u, -1))
            inv = recip(t)
            cs[r + i, 0] = inv + jnp.maximum(rows[i + 4] - u, 0.0) * inv
            cs[r + i, 1] = inv + jnp.maximum(rows[i] - u, 0.0) * inv
            cs[r + i, 2] = inv + jnp.maximum(roll(u, -2) - u, 0.0) * inv
            cs[r + i, 3] = inv + jnp.maximum(roll(u, 2) - u, 0.0) * inv
        return carry

    row_loop(PAD + 6, ROWS - 2 * (PAD + 6), weigh)

    src = dx
    for n in range(5):
        dst = da if n % 2 == 0 else db
        margin = 6 + n

        def body(r, total, src=src, dst=dst, last=n == 4):
            rows = [src[r - 1 + i] for i in range(BLOCK + 2)]
            for i in range(BLOCK):
                u = rows[i + 1]
                fresh = (
                    cs[r + i, 0] * rows[i + 2]
                    + cs[r + i, 1] * rows[i]
                    + cs[r + i, 2] * roll(u, -1)
                    + cs[r + i, 3] * roll(u, 1)
                )
                dst[r + i] = fresh
                if last:
                    total = total + fresh
            return total

        mass = row_loop(PAD + margin, ROWS - 2 * (PAD + margin), body, jnp.zeros((SUB, 128), F32))
        src = dst
    sums[...] = to_row([own(total5, 4), own(mass, 10)])
    transpose_out(w5, scratch, value)
    transpose_out(src, scratch, density)


def finish_kernel(value_in, density_in, row1, row2, row3, value, density, ergodic):
    _, lam2, _ = first_means(row1[...])
    _, lam4, _ = second_means(row2[...], lam2)
    shift = from_row(row3[...], 0) * (1.0 / CELLS)
    scale = CELLS / from_row(row3[...], 1)
    ergodic[...] = to_row([lam4 + 2.0 * shift])
    for k in range(K):
        value[k] = value_in[k] - shift[k : k + 1]
        density[k] = density_in[k] * scale[k : k + 1]


VMEM = pl.BlockSpec(memory_space=pltpu.VMEM)
SMEM = pl.BlockSpec(memory_space=pltpu.SMEM)


def kernel(body, outs, ins, scratch=(), aliases=None):
    return pl.pallas_call(
        body,
        out_shape=[jax.ShapeDtypeStruct(shape, F32) for shape in outs],
        in_specs=ins,
        out_specs=[VMEM] * len(outs),
        scratch_shapes=[pltpu.VMEM(shape, F32) for shape in scratch],
        input_output_aliases=aliases or {},
        compiler_params=pltpu.CompilerParams(vmem_limit_bytes=48 * 1024 * 1024),
    )


def exchange(low, high, axes, count):
    before = lax.ppermute(high, axes, [(i, (i + 1) % count) for i in range(count)])
    after = lax.ppermute(low, axes, [((i + 1) % count, i) for i in range(count)])
    return before, after


def total_over_devices(row):
    rows = jnp.broadcast_to(row[None], (DEVICES, 1, 128))
    return jnp.sum(lax.all_to_all(rows, AXES, 0, 0), axis=0)


def shards(cost, density_start, coupling):
    big = (ROWS, SUB, 128)
    row = (1, 128)
    strip = (HALO + D_HALO, K, 128)
    sx, dx, top, bottom, to_left, to_right = kernel(
        source_kernel, [big, big, strip, strip, (32, 8, 128), (32, 8, 128)], [SMEM, VMEM, VMEM]
    )(coupling, cost, density_start)
    above, below = exchange(top, bottom, GX, 16)
    from_left, from_right = exchange(to_left, to_right, GY, 16)
    sx, dx, to_left, to_right, sums = kernel(
        first_sums_kernel, [big, big, (5, 8, 128), (5, 8, 128), row], [VMEM] * 6, aliases={0: 0, 1: 1}
    )(sx, dx, above, below, from_left, from_right)
    from_left, from_right = exchange(to_left, to_right, GY, 16)
    row1 = total_over_devices(sums)
    sx, dx, w3, sums = kernel(
        second_sums_kernel, [big, big, big, row], [VMEM] * 5, scratch=[big, big], aliases={0: 0, 1: 1}
    )(sx, dx, from_left, from_right, row1)
    row2 = total_over_devices(sums)
    block = (K, N, N)
    value, density, sums = kernel(
        last_sums_kernel,
        [block, block, row],
        [VMEM] * 5,
        scratch=[big, big, (ROWS, 4, SUB, 128), big, big, (N, K, 128)],
    )(sx, dx, w3, row1, row2)
    row3 = total_over_devices(sums)
    value, density, ergodic = kernel(finish_kernel, [block, block, row], [VMEM] * 5)(
        value, density, row1, row2, row3
    )
    return value, density, ergodic[0, :K]


def solution(mesh):
    torus = Mesh(mesh.devices.reshape(4, 2, 2, 2, 8), AXES)
    specs = (P(None, GX, GY), P(None, GX, GY), P())
    return jax.shard_map(shards, mesh=torus, in_specs=specs, out_specs=specs, check_vma=False)
```

```python
import functools

import jax
import jax.numpy as jnp
from jax import lax
from jax.experimental import pallas as pl
from jax.experimental.pallas import tpu as pltpu
from jax.sharding import Mesh
from jax.sharding import PartitionSpec as P

HALO = 10
D_HALO = 5
PAD = 4
ROW0 = PAD + HALO
N = 128
ROWS = N + 2 * ROW0
K = 16
SUB = 24
AXES = ("y", "xh", "c", "xl", "z")
GX = ("y", "xh", "c")
GY = ("xl", "z")
DEVICES = 256
CELLS = 2048.0 * 2048.0
SLOT = (0, 16, 64, 80)
BLOCK = 32
GROUPS = 4
F32 = jnp.float32


def lanes(shape):
    return lax.broadcasted_iota(jnp.int32, shape, 1)


def roll(x, shift):
    return pltpu.roll(x, shift % 128, 1)


def between(lane, low, high):
    return (lane >= low) & (lane < high)


def recip(x):
    return 1.0 / x


def pack(rows, left):
    lane = lanes((8, 128))
    out = jnp.zeros((8, 128), F32)
    for (s0, s1, d0, d1), base in zip(rows, SLOT):
        for half, (s, d) in enumerate(((s0, d0), (s1, d1))):
            at = base + 32 * half
            ds = roll(s, at if left else at + HALO)
            dd = roll(d, at + HALO if left else at + HALO + D_HALO)
            out = jnp.where(between(lane, at, at + HALO), ds, out)
            out = jnp.where(between(lane, at + HALO, at + HALO + D_HALO), dd, out)
    return out


def windows(a, b):
    lane = lanes((8, 128))
    left = jnp.where(lane < 32, roll(a, 10), roll(b, 42))
    right = jnp.where(lane < 96, roll(a, 86), roll(b, 118))
    return jnp.where(lane < 64, left, right)


def halo_masks():
    lane = lanes((8, 128))
    left = between(lane, 0, 10) | between(lane, 32, 42)
    right = between(lane, 86, 96) | between(lane, 118, 128)
    return left, right


def beyond(window, from_left, from_right, i, masks, density):
    base = SLOT[i]
    a = roll(from_left, -base - 5 if density else -base)
    b = roll(from_right, 76 - base if density else 86 - base)
    return jnp.where(masks[0], a, jnp.where(masks[1], b, window))


def own(total, margin):
    lane = lanes((K, 128))
    main = jnp.where(between(lane, margin, N - margin), total[:K], 0.0)
    main = jnp.sum(main, axis=1, keepdims=True)
    if margin == 0:
        return main
    edge = total[K:]
    lane = lanes((8, 128))
    halves = []
    for half in range(2):
        at = 32 * half
        mask = between(lane, at + 10, at + 10 + margin) | between(lane, 64 + at + 22 - margin, 64 + at + 22)
        halves.append(jnp.sum(jnp.where(mask, edge, 0.0), axis=1, keepdims=True))
    return main + jnp.concatenate(halves, axis=0)


def to_row(columns):
    lane, cls = lanes((K, 128)), lax.broadcasted_iota(jnp.int32, (K, 128), 0)
    grid = jnp.zeros((K, 128), F32)
    for i, column in enumerate(columns):
        grid = jnp.where(lane == cls + K * i, column, grid)
    return jnp.sum(grid, axis=0, keepdims=True)


def from_row(row, i):
    lane, cls = lanes((K, 128)), lax.broadcasted_iota(jnp.int32, (K, 128), 0)
    return jnp.sum(jnp.where(lane == cls + K * i, row, 0.0), axis=1, keepdims=True)


def spread(column):
    wide = jnp.broadcast_to(column, (K, 128))
    lane = lanes((8, 128))
    edge = jnp.where((lane // 32) % 2 == 0, wide[:8], wide[8:])
    return jnp.concatenate([wide, edge], axis=0)


def parts(up, mid, down, s):
    left, right = roll(mid, 1), roll(mid, -1)
    px = 2.0 + jnp.abs(up - down)
    py = 2.0 + jnp.abs(left - right)
    n = s + (px * (2.0 * (up + down) + (4.0 - px)) + py * (2.0 * (left + right) + (4.0 - py)))
    return n, recip(px + py)


def row_loop(first, count, body, init=0, block=None):
    blocks = -(-count // (block or BLOCK))
    size = -(-count // blocks)
    first = first - (blocks * size - count) // 2

    def step(i, carry):
        return body(first + i * size, size, carry)

    return lax.fori_loop(0, blocks, step, init)


def sweep(src, s_ref, dst, lam8, minus, margin, summed=False):
    def body(r, size, total):
        rows = [src[r - 1 + i] for i in range(size + 2)]
        for i in range(size):
            n, inv = parts(rows[i], rows[i + 1], rows[i + 2], s_ref[r + i] - lam8)
            w = n * (0.25 * inv)
            if minus is not None:
                w = w - minus
            dst[r + i] = w
        return total

    row_loop(PAD + margin, ROWS - 2 * (PAD + margin), body)
    if summed:
        def add(r, size, total):
            for i in range(size):
                total = total + dst[r + i]
            return total

        return row_loop(ROW0, N, add, jnp.zeros((SUB, 128), F32))


def sweep_sums(src, s_ref, half):
    def body(r, size, carry):
        a, b = carry
        rows = [src[r - 1 + i] for i in range(size + 2)]
        if half:
            rows = [row * 0.0625 + 0.5 for row in rows]
        for i in range(size):
            n, inv = parts(rows[i], rows[i + 1], rows[i + 2], s_ref[r + i])
            a = a + n * inv
            b = b + inv
        return a, b

    zero = jnp.zeros((SUB, 128), F32)
    return row_loop(ROW0, N, body, (zero, zero))


def source_kernel(c_ref, cost_ref, d_ref, sx, dx, top, bottom, to_left, to_right):
    s2, d2 = sx.reshape(ROWS * SUB, 128), dx.reshape(ROWS * SUB, 128)

    def chunk(i, carry):
        r = pl.multiple_of(i * 8, 8)
        dens = [d_ref[j, pl.ds(r, 8), :] for j in range(K)]
        base = (ROW0 + r) * SUB
        for j in range(K):
            d2[pl.ds(base + j, 8, stride=SUB), :] = dens[j]
        for k in range(K):
            acc = cost_ref[k, pl.ds(r, 8), :]
            for j in range(K):
                acc = acc + c_ref[k, j] * dens[j]
            s2[pl.ds(base + k, 8, stride=SUB), :] = acc * 8.0 - 8.0
        return carry

    lax.fori_loop(0, N // 8, chunk, 0)

    def group(g0, carry):
        for g in range(GROUPS):
            g = g0 * GROUPS + g
            r = ROW0 + g * 4
            rows = [(sx[r + i, 0:8], sx[r + i, 8:16], dx[r + i, 0:8], dx[r + i, 8:16]) for i in range(4)]
            to_left[g] = pack(rows, True)
            to_right[g] = pack(rows, False)
        return carry

    lax.fori_loop(0, N // 4 // GROUPS, group, 0)
    for i in range(HALO):
        top[i] = sx[ROW0 + i, 0:K]
        bottom[i] = sx[ROW0 + N - HALO + i, 0:K]
    for i in range(D_HALO):
        top[HALO + i] = dx[ROW0 + i, 0:K]
        bottom[HALO + i] = dx[ROW0 + N - D_HALO + i, 0:K]


def halo_rows():
    return [(i, PAD + i) for i in range(HALO)] + [(HALO + i, ROW0 + N + i) for i in range(HALO)]


def first_sums_kernel(s_in, d_in, above, below, from_left, from_right, sx, dx, to_left, to_right, sums):
    del s_in, d_in
    for i in range(HALO):
        sx[PAD + i, 0:K] = above[i]
        sx[ROW0 + N + i, 0:K] = below[i]
    for i in range(D_HALO):
        dx[ROW0 - D_HALO + i, 0:K] = above[HALO + i]
        dx[ROW0 + N + i, 0:K] = below[HALO + i]
    zero = jnp.zeros((8, 128), F32)
    tiles = []
    for i in range(HALO):
        d = above[HALO + i - (HALO - D_HALO)] if i >= HALO - D_HALO else None
        tiles.append((above[i], d, PAD + i))
    for i in range(HALO):
        d = below[HALO + i] if i < D_HALO else None
        tiles.append((below[i], d, ROW0 + N + i))
    packed = []
    for s, d, at in tiles:
        sx[at, K:SUB] = windows(s[:8], s[8:])
        if d is not None:
            dx[at, K:SUB] = windows(d[:8], d[8:])
            packed.append((s[:8], s[8:], d[:8], d[8:]))
        else:
            packed.append((s[:8], s[8:], zero, zero))
    for g in range(5):
        to_left[g] = pack(packed[4 * g : 4 * g + 4], True)
        to_right[g] = pack(packed[4 * g : 4 * g + 4], False)

    masks = halo_masks()

    def group(g0, total):
        for g in range(GROUPS):
            g = g0 * GROUPS + g
            r = ROW0 + g * 4
            fl, fr = from_left[g], from_right[g]
            for i in range(4):
                s = sx[r + i, 0:K]
                total = total + s
                sx[r + i, K:SUB] = beyond(windows(s[:8], s[8:]), fl, fr, i, masks, False)
                d = dx[r + i, 0:K]
                dx[r + i, K:SUB] = beyond(windows(d[:8], d[8:]), fl, fr, i, masks, True)
        return total

    total = lax.fori_loop(0, N // 4 // GROUPS, group, jnp.zeros((K, 128), F32))
    a, b = sweep_sums(sx, sx, True)
    sums[...] = to_row([jnp.sum(total, axis=1, keepdims=True), own(a, 1), own(b, 1)])


def first_means(row):
    lam1 = from_row(row, 0) * (0.125 / CELLS) + 1.0
    mean2 = from_row(row, 1) * (0.25 / CELLS) - lam1 * (from_row(row, 2) * (2.0 / CELLS))
    return lam1, 2.0 * mean2, mean2


def second_means(row, lam2):
    lam3 = lam2 + from_row(row, 0) * (2.0 / CELLS)
    mean4 = from_row(row, 1) * (0.25 / CELLS) - lam3 * (from_row(row, 2) * (2.0 / CELLS))
    return lam3, lam2 + 2.0 * mean4, mean4


def second_sums_kernel(s_in, d_in, from_left, from_right, row1, sx, dx, w3, sums, w1, v2):
    del s_in, d_in
    masks = halo_masks()
    for i, at in halo_rows():
        fl, fr = from_left[i // 4], from_right[i // 4]
        sx[at, K:SUB] = beyond(sx[at, K:SUB], fl, fr, i % 4, masks, False)
        if HALO - D_HALO <= i < HALO + D_HALO:
            dx[at, K:SUB] = beyond(dx[at, K:SUB], fl, fr, i % 4, masks, True)

    def start(r, size, carry):
        for i in range(size):
            w1[r + i] = sx[r + i] * 0.0625 + 0.5
        return carry

    row_loop(PAD, ROWS - 2 * PAD, start)
    lam1, lam2, mean2 = first_means(row1[...])
    sweep(w1, sx, v2, spread(8.0 * lam1), spread(mean2), 1)
    total = sweep(v2, sx, w3, spread(8.0 * lam2), None, 2, True)
    a, b = sweep_sums(w3, sx, False)
    sums[...] = to_row([own(total, 2), own(a, 3), own(b, 3)])


def transpose_out(src, scratch, out):
    lane = lanes((8, 128))
    low, high = lane < 10, lane >= 118

    def body(g, carry):
        for i in range(BLOCK):
            r = g * BLOCK + i
            e = src[ROW0 + r, K:SUB]
            for half in range(2):
                a = src[ROW0 + r, 8 * half : 8 * half + 8]
                left = roll(e, -10 - 32 * half)
                right = roll(e, 42 - 32 * half)
                scratch[r, 8 * half : 8 * half + 8] = jnp.where(low, left, jnp.where(high, right, a))
        return carry

    lax.fori_loop(0, N // BLOCK, body, 0)
    flat = scratch.reshape(N * K, 128)

    def chunk(i, carry):
        for j in range(4):
            r = pl.multiple_of(i * 32 + j * 8, 8)
            for k in range(K):
                out[k, pl.ds(r, 8), :] = flat[pl.ds(r * K + k, 8, stride=K), :]
        return carry

    lax.fori_loop(0, N // 32, chunk, 0)


def weigh(w5, cs):
    def body(r, size, carry):
        rows = [w5[r - 2 + i] for i in range(size + 4)]
        for i in range(size):
            u = rows[i + 2]
            t = 4.0 + jnp.abs(rows[i + 1] - rows[i + 3]) + jnp.abs(roll(u, 1) - roll(u, -1))
            inv = recip(t)
            cs[r + i, 0] = inv + jnp.maximum(rows[i + 4] - u, 0.0) * inv
            cs[r + i, 1] = inv + jnp.maximum(rows[i] - u, 0.0) * inv
            cs[r + i, 2] = inv + jnp.maximum(roll(u, -2) - u, 0.0) * inv
            cs[r + i, 3] = inv + jnp.maximum(roll(u, 2) - u, 0.0) * inv
        return carry

    row_loop(PAD + 6, ROWS - 2 * (PAD + 6), body)


def fp(src, dst, cs, margin, summed):
    def body(r, size, total):
        rows = [src[r - 1 + i] for i in range(size + 2)]
        for i in range(size):
            u = rows[i + 1]
            fresh = (
                cs[r + i, 0] * rows[i + 2]
                + cs[r + i, 1] * rows[i]
                + cs[r + i, 2] * roll(u, -1)
                + cs[r + i, 3] * roll(u, 1)
            )
            dst[r + i] = fresh
            if summed:
                total = total + fresh
        return total

    return row_loop(PAD + margin, ROWS - 2 * (PAD + margin), body, jnp.zeros((SUB, 128), F32))


def last_sums_kernel(sx, dx, w3, row1, row2, value, density, sums, v4, w5, cs, da, db, scratch):
    _, lam2, _ = first_means(row1[...])
    lam3, lam4, mean4 = second_means(row2[...], lam2)
    sweep(w3, sx, v4, spread(8.0 * lam3), spread(mean4), 3)
    total5 = sweep(v4, sx, w5, spread(8.0 * lam4), None, 4, True)

    weigh(w5, cs)
    src = dx
    for n in range(5):
        dst = da if n % 2 == 0 else db
        mass = fp(src, dst, cs, 6 + n, n == 4)
        src = dst
    sums[...] = to_row([own(total5, 4), own(mass, 10)])
    transpose_out(w5, scratch, value)
    transpose_out(src, scratch, density)


def finish_kernel(value_in, density_in, row1, row2, row3, value, density, ergodic):
    _, lam2, _ = first_means(row1[...])
    _, lam4, _ = second_means(row2[...], lam2)
    shift = from_row(row3[...], 0) * (1.0 / CELLS)
    scale = CELLS / from_row(row3[...], 1)
    ergodic[...] = to_row([lam4 + 2.0 * shift])
    for k in range(K):
        value[k] = value_in[k] - shift[k : k + 1]
        density[k] = density_in[k] * scale[k : k + 1]


VMEM = pl.BlockSpec(memory_space=pltpu.VMEM)
SMEM = pl.BlockSpec(memory_space=pltpu.SMEM)


def kernel(body, outs, ins, scratch=(), aliases=None, vmem=16):
    return pl.pallas_call(
        body,
        out_shape=[jax.ShapeDtypeStruct(shape, F32) for shape in outs],
        in_specs=ins,
        out_specs=[VMEM] * len(outs),
        scratch_shapes=[pltpu.VMEM(shape, F32) for shape in scratch],
        input_output_aliases=aliases or {},
        compiler_params=pltpu.CompilerParams(vmem_limit_bytes=vmem * 1024 * 1024),
    )


def exchange(low, high, axes, count):
    before = lax.ppermute(high, axes, [(i, (i + 1) % count) for i in range(count)])
    after = lax.ppermute(low, axes, [((i + 1) % count, i) for i in range(count)])
    return before, after


def total_over_devices(row):
    rows = jnp.broadcast_to(row[None], (DEVICES, 1, 128))
    return jnp.sum(lax.all_to_all(rows, AXES, 0, 0), axis=0)


def shards(cost, density_start, coupling):
    big = (ROWS, SUB, 128)
    row = (1, 128)
    strip = (HALO + D_HALO, K, 128)
    sx, dx, top, bottom, to_left, to_right = kernel(
        source_kernel, [big, big, strip, strip, (32, 8, 128), (32, 8, 128)], [SMEM, VMEM, VMEM]
    )(coupling, cost, density_start)
    above, below = exchange(top, bottom, GX, 16)
    from_left, from_right = exchange(to_left, to_right, GY, 16)
    sx, dx, to_left, to_right, sums = kernel(
        first_sums_kernel, [big, big, (5, 8, 128), (5, 8, 128), row], [VMEM] * 6, aliases={0: 0, 1: 1}
    )(sx, dx, above, below, from_left, from_right)
    from_left, from_right = exchange(to_left, to_right, GY, 16)
    row1 = total_over_devices(sums)
    sx, dx, w3, sums = kernel(
        second_sums_kernel, [big, big, big, row], [VMEM] * 5, scratch=[big, big], aliases={0: 0, 1: 1}
    )(sx, dx, from_left, from_right, row1)
    row2 = total_over_devices(sums)
    block = (K, N, N)
    value, density, sums = kernel(
        last_sums_kernel,
        [block, block, row],
        [VMEM] * 5,
        scratch=[big, big, (ROWS, 4, SUB, 128), big, big, (N, K, 128)],
        vmem=32,
    )(sx, dx, w3, row1, row2)
    row3 = total_over_devices(sums)
    value, density, ergodic = kernel(finish_kernel, [block, block, row], [VMEM] * 5)(
        value, density, row1, row2, row3
    )
    return value, density, ergodic[0, :K]


def solution(mesh):
    torus = Mesh(mesh.devices.reshape(4, 2, 2, 2, 8), AXES)
    specs = (P(None, GX, GY), P(None, GX, GY), P())
    return jax.shard_map(shards, mesh=torus, in_specs=specs, out_specs=specs, check_vma=False)
```

```python
import functools

import jax
import jax.numpy as jnp
from jax import lax
from jax.experimental import pallas as pl
from jax.experimental.pallas import tpu as pltpu
from jax.sharding import Mesh
from jax.sharding import PartitionSpec as P

HALO = 10
D_HALO = 5
PAD = 4
ROW0 = PAD + HALO
N = 128
ROWS = N + 2 * ROW0
K = 16
SUB = 24
AXES = ("y", "xh", "c", "xl", "z")
GX = ("y", "xh", "c")
GY = ("xl", "z")
DEVICES = 256
CELLS = 2048.0 * 2048.0
SLOT = (0, 16, 64, 80)
BLOCK = 32
GROUPS = 4
CHUNK = 16
WAVE = 29
F32 = jnp.float32


def lanes(shape):
    return lax.broadcasted_iota(jnp.int32, shape, 1)


def roll(x, shift):
    return pltpu.roll(x, shift % 128, 1)


def between(lane, low, high):
    return (lane >= low) & (lane < high)


def recip(x):
    return 1.0 / x


def pack(rows, left):
    lane = lanes((8, 128))
    out = jnp.zeros((8, 128), F32)
    for (s0, s1, d0, d1), base in zip(rows, SLOT):
        for half, (s, d) in enumerate(((s0, d0), (s1, d1))):
            at = base + 32 * half
            ds = roll(s, at if left else at + HALO)
            dd = roll(d, at + HALO if left else at + HALO + D_HALO)
            out = jnp.where(between(lane, at, at + HALO), ds, out)
            out = jnp.where(between(lane, at + HALO, at + HALO + D_HALO), dd, out)
    return out


def windows(a, b):
    lane = lanes((8, 128))
    left = jnp.where(lane < 32, roll(a, 10), roll(b, 42))
    right = jnp.where(lane < 96, roll(a, 86), roll(b, 118))
    return jnp.where(lane < 64, left, right)


def halo_masks():
    lane = lanes((8, 128))
    left = between(lane, 0, 10) | between(lane, 32, 42)
    right = between(lane, 86, 96) | between(lane, 118, 128)
    return left, right


def beyond(window, from_left, from_right, i, masks, density):
    base = SLOT[i]
    a = roll(from_left, -base - 5 if density else -base)
    b = roll(from_right, 76 - base if density else 86 - base)
    return jnp.where(masks[0], a, jnp.where(masks[1], b, window))


def own(total, margin):
    lane = lanes((K, 128))
    main = jnp.where(between(lane, margin, N - margin), total[:K], 0.0)
    main = jnp.sum(main, axis=1, keepdims=True)
    if margin == 0:
        return main
    edge = total[K:]
    lane = lanes((8, 128))
    halves = []
    for half in range(2):
        at = 32 * half
        mask = between(lane, at + 10, at + 10 + margin) | between(lane, 64 + at + 22 - margin, 64 + at + 22)
        halves.append(jnp.sum(jnp.where(mask, edge, 0.0), axis=1, keepdims=True))
    return main + jnp.concatenate(halves, axis=0)


def to_row(columns):
    lane, cls = lanes((K, 128)), lax.broadcasted_iota(jnp.int32, (K, 128), 0)
    grid = jnp.zeros((K, 128), F32)
    for i, column in enumerate(columns):
        grid = jnp.where(lane == cls + K * i, column, grid)
    return jnp.sum(grid, axis=0, keepdims=True)


def from_row(row, i):
    lane, cls = lanes((K, 128)), lax.broadcasted_iota(jnp.int32, (K, 128), 0)
    return jnp.sum(jnp.where(lane == cls + K * i, row, 0.0), axis=1, keepdims=True)


def spread(column):
    wide = jnp.broadcast_to(column, (K, 128))
    lane = lanes((8, 128))
    edge = jnp.where((lane // 32) % 2 == 0, wide[:8], wide[8:])
    return jnp.concatenate([wide, edge], axis=0)


def parts(up, mid, down, s):
    left, right = roll(mid, 1), roll(mid, -1)
    px = 2.0 + jnp.abs(up - down)
    py = 2.0 + jnp.abs(left - right)
    n = s + (px * (2.0 * (up + down) + (4.0 - px)) + py * (2.0 * (left + right) + (4.0 - py)))
    return n, recip(px + py)


def row_loop(first, count, body, init=0, before=None):
    blocks = -(-count // BLOCK)
    size = -(-count // blocks)
    first = first - (blocks * size - count) // 2

    def step(i, carry):
        if before is not None:
            before(i)
        return body(first + i * size, size, carry)

    return lax.fori_loop(0, blocks, step, init)


def sweep(src, s_ref, dst, lam8, minus, margin, summed=False, before=None):
    def body(r, size, total):
        rows = [src[r - 1 + i] for i in range(size + 2)]
        for i in range(size):
            n, inv = parts(rows[i], rows[i + 1], rows[i + 2], s_ref[r + i] - lam8)
            w = n * (0.25 * inv)
            if minus is not None:
                w = w - minus
            dst[r + i] = w
        return total

    row_loop(PAD + margin, ROWS - 2 * (PAD + margin), body, before=before)
    if summed:
        def add(r, size, total):
            for i in range(size):
                total = total + dst[r + i]
            return total

        return row_loop(ROW0, N, add, jnp.zeros((SUB, 128), F32))


def sweep_sums(src, s_ref, half):
    def body(r, size, carry):
        a, b = carry
        rows = [src[r - 1 + i] for i in range(size + 2)]
        if half:
            rows = [row * 0.0625 + 0.5 for row in rows]
        for i in range(size):
            n, inv = parts(rows[i], rows[i + 1], rows[i + 2], s_ref[r + i])
            a = a + n * inv
            b = b + inv
        return a, b

    zero = jnp.zeros((SUB, 128), F32)
    return row_loop(ROW0, N, body, (zero, zero))


def source_kernel(c_hbm, cost_hbm, d_hbm, sx, dx, top, bottom, to_left, to_right, c_ref, cost_ref, d_ref, sems, c_sem):
    s2, d2 = sx.reshape(ROWS * SUB, 128), dx.reshape(ROWS * SUB, 128)
    coupling = pltpu.make_async_copy(c_hbm, c_ref, c_sem)
    coupling.start()

    def copies(i):
        part = pl.ds(pl.multiple_of(i * CHUNK, CHUNK), CHUNK)
        return (
            pltpu.make_async_copy(d_hbm.at[:, part], d_ref.at[:, part], sems.at[0, i]),
            pltpu.make_async_copy(cost_hbm.at[:, part], cost_ref.at[:, part], sems.at[1, i]),
        )

    for i in range(N // CHUNK):
        for copy in copies(i):
            copy.start()
    coupling.wait()

    def chunk(i, carry):
        for copy in copies(i):
            copy.wait()
        for part in range(CHUNK // 8):
            r = pl.multiple_of(i * CHUNK + part * 8, 8)
            dens = [d_ref[j, pl.ds(r, 8), :] for j in range(K)]
            base = (ROW0 + r) * SUB
            for j in range(K):
                d2[pl.ds(base + j, 8, stride=SUB), :] = dens[j]
            for k in range(K):
                acc = cost_ref[k, pl.ds(r, 8), :]
                for j in range(K):
                    acc = acc + c_ref[k, j] * dens[j]
                s2[pl.ds(base + k, 8, stride=SUB), :] = acc * 8.0 - 8.0
        return carry

    lax.fori_loop(0, N // CHUNK, chunk, 0)

    def group(g0, carry):
        for g in range(GROUPS):
            g = g0 * GROUPS + g
            r = ROW0 + g * 4
            rows = [(sx[r + i, 0:8], sx[r + i, 8:16], dx[r + i, 0:8], dx[r + i, 8:16]) for i in range(4)]
            to_left[g] = pack(rows, True)
            to_right[g] = pack(rows, False)
        return carry

    lax.fori_loop(0, N // 4 // GROUPS, group, 0)
    for i in range(HALO):
        top[i] = sx[ROW0 + i, 0:K]
        bottom[i] = sx[ROW0 + N - HALO + i, 0:K]
    for i in range(D_HALO):
        top[HALO + i] = dx[ROW0 + i, 0:K]
        bottom[HALO + i] = dx[ROW0 + N - D_HALO + i, 0:K]


def halo_rows():
    return [(i, PAD + i) for i in range(HALO)] + [(HALO + i, ROW0 + N + i) for i in range(HALO)]


def first_sums_kernel(s_in, d_in, above, below, from_left, from_right, sx, dx, d_hbm, to_left, to_right, sums, d_sem):
    del s_in, d_in
    zero = jnp.zeros((8, 128), F32)
    masks = halo_masks()
    packed = []
    for i, at in halo_rows():
        strip = above if i < HALO else below
        s = strip[i % HALO]
        sx[at, 0:K] = s
        sx[at, K:SUB] = windows(s[:8], s[8:])
        if HALO - D_HALO <= i < HALO + D_HALO:
            d = strip[HALO + i % D_HALO]
            dx[at, 0:K] = d
            dx[at, K:SUB] = windows(d[:8], d[8:])
            packed.append((s[:8], s[8:], d[:8], d[8:]))
        else:
            packed.append((s[:8], s[8:], zero, zero))
    for g in range(5):
        to_left[g] = pack(packed[4 * g : 4 * g + 4], True)
        to_right[g] = pack(packed[4 * g : 4 * g + 4], False)

    def d_group(g0, carry):
        for g in range(GROUPS):
            g = g0 * GROUPS + g
            fl, fr = from_left[g], from_right[g]
            for i in range(4):
                r = ROW0 + g * 4 + i
                d = dx[r, 0:K]
                dx[r, K:SUB] = beyond(windows(d[:8], d[8:]), fl, fr, i, masks, True)
        return carry

    lax.fori_loop(0, N // 4 // GROUPS, d_group, 0)
    used = pl.ds(ROW0 - D_HALO - 1, N + 2 * D_HALO + 2)
    store_d = pltpu.make_async_copy(dx.at[used], d_hbm.at[used], d_sem)
    store_d.start()

    def group(g0, total):
        for g in range(GROUPS):
            g = g0 * GROUPS + g
            fl, fr = from_left[g], from_right[g]
            for i in range(4):
                r = ROW0 + g * 4 + i
                s = sx[r, 0:K]
                total = total + s
                sx[r, K:SUB] = beyond(windows(s[:8], s[8:]), fl, fr, i, masks, False)
        return total

    total = lax.fori_loop(0, N // 4 // GROUPS, group, jnp.zeros((K, 128), F32))
    a, b = sweep_sums(sx, sx, True)
    sums[...] = to_row([jnp.sum(total, axis=1, keepdims=True), own(a, 1), own(b, 1)])
    store_d.wait()


def first_means(row):
    lam1 = from_row(row, 0) * (0.125 / CELLS) + 1.0
    mean2 = from_row(row, 1) * (0.25 / CELLS) - lam1 * (from_row(row, 2) * (2.0 / CELLS))
    return lam1, 2.0 * mean2, mean2


def second_means(row, lam2):
    lam3 = lam2 + from_row(row, 0) * (2.0 / CELLS)
    mean4 = from_row(row, 1) * (0.25 / CELLS) - lam3 * (from_row(row, 2) * (2.0 / CELLS))
    return lam3, lam2 + 2.0 * mean4, mean4


def second_sums_kernel(s_in, from_left, from_right, row1, sx, w3_hbm, sums, w1, v2, w3, sem):
    del s_in
    masks = halo_masks()
    for i, at in halo_rows():
        sx[at, K:SUB] = beyond(sx[at, K:SUB], from_left[i // 4], from_right[i // 4], i % 4, masks, False)

    def start(r, size, carry):
        for i in range(size):
            w1[r + i] = sx[r + i] * 0.0625 + 0.5
        return carry

    row_loop(PAD, ROWS - 2 * PAD, start)
    lam1, lam2, mean2 = first_means(row1[...])
    sweep(w1, sx, v2, spread(8.0 * lam1), spread(mean2), 1)
    total = sweep(v2, sx, w3, spread(8.0 * lam2), None, 2, True)
    store = pltpu.make_async_copy(w3, w3_hbm, sem)
    store.start()
    a, b = sweep_sums(w3, sx, False)
    sums[...] = to_row([own(total, 2), own(a, 3), own(b, 3)])
    store.wait()


def transpose_out(src, scratch, out):
    lane = lanes((8, 128))
    low, high = lane < 10, lane >= 118

    def body(g, carry):
        for i in range(BLOCK):
            r = g * BLOCK + i
            e = src[ROW0 + r, K:SUB]
            for half in range(2):
                a = src[ROW0 + r, 8 * half : 8 * half + 8]
                left = roll(e, -10 - 32 * half)
                right = roll(e, 42 - 32 * half)
                scratch[r, 8 * half : 8 * half + 8] = jnp.where(low, left, jnp.where(high, right, a))
        return carry

    lax.fori_loop(0, N // BLOCK, body, 0)
    flat = scratch.reshape(N * K, 128)

    def chunk(i, carry):
        for j in range(4):
            r = pl.multiple_of(i * 32 + j * 8, 8)
            for k in range(K):
                out[k, pl.ds(r, 8), :] = flat[pl.ds(r * K + k, 8, stride=K), :]
        return carry

    lax.fori_loop(0, N // 32, chunk, 0)


def weigh(w5, cs):
    def body(r, size, carry):
        rows = [w5[r - 2 + i] for i in range(size + 4)]
        for i in range(size):
            u = rows[i + 2]
            t = 4.0 + jnp.abs(rows[i + 1] - rows[i + 3]) + jnp.abs(roll(u, 1) - roll(u, -1))
            inv = recip(t)
            cs[r + i, 0] = inv + jnp.maximum(rows[i + 4] - u, 0.0) * inv
            cs[r + i, 1] = inv + jnp.maximum(rows[i] - u, 0.0) * inv
            cs[r + i, 2] = inv + jnp.maximum(roll(u, -2) - u, 0.0) * inv
            cs[r + i, 3] = inv + jnp.maximum(roll(u, 2) - u, 0.0) * inv
        return carry

    row_loop(PAD + 6, ROWS - 2 * (PAD + 6), body)


def fp(src, dst, cs, margin, summed):
    def body(r, size, total):
        rows = [src[r - 1 + i] for i in range(size + 2)]
        for i in range(size):
            u = rows[i + 1]
            fresh = (
                cs[r + i, 0] * rows[i + 2]
                + cs[r + i, 1] * rows[i]
                + cs[r + i, 2] * roll(u, -1)
                + cs[r + i, 3] * roll(u, 1)
            )
            dst[r + i] = fresh
            if summed:
                total = total + fresh
        return total

    return row_loop(PAD + margin, ROWS - 2 * (PAD + margin), body, jnp.zeros((SUB, 128), F32))


def last_sums_kernel(
    sx, d_hbm, w3_hbm, from_left, from_right, row1, row2, value_hbm, density, sums,
    w3, v4, w5, cs, dx, da, db, scratch, value, w3_sems, d_sem, value_sem,
):
    size = WAVE
    first = PAD + 2
    copies = [pltpu.make_async_copy(w3_hbm.at[pl.ds(0, first + 1)], w3.at[pl.ds(0, first + 1)], w3_sems.at[5])]

    def wave(i):
        part = pl.ds(first + 1 + i * size, size)
        return pltpu.make_async_copy(w3_hbm.at[part], w3.at[part], w3_sems.at[i])

    head = copies[0]
    head.start()
    for i in range(5):
        wave(i).start()
    used = pl.ds(ROW0 - D_HALO - 1, N + 2 * D_HALO + 2)
    load_d = pltpu.make_async_copy(d_hbm.at[used], dx.at[used], d_sem)
    load_d.start()
    _, lam2, _ = first_means(row1[...])
    lam3, lam4, mean4 = second_means(row2[...], lam2)
    head.wait()
    sweep(w3, sx, v4, spread(8.0 * lam3), spread(mean4), 3, before=lambda i: wave(i).wait())
    total5 = sweep(v4, sx, w5, spread(8.0 * lam4), None, 4, True)
    transpose_out(w5, scratch, value)
    store = pltpu.make_async_copy(value, value_hbm, value_sem)
    store.start()
    weigh(w5, cs)
    load_d.wait()
    masks = halo_masks()
    for i, at in halo_rows():
        if HALO - D_HALO <= i < HALO + D_HALO:
            dx[at, K:SUB] = beyond(dx[at, K:SUB], from_left[i // 4], from_right[i // 4], i % 4, masks, True)
    src = dx
    for n in range(5):
        dst = da if n % 2 == 0 else db
        mass = fp(src, dst, cs, 6 + n, n == 4)
        src = dst
    sums[...] = to_row([own(total5, 4), own(mass, 10)])
    transpose_out(src, scratch, density)
    store.wait()


def finish_kernel(
    value_hbm, density_in, row1, row2, row3, value_out, density_out, ergodic, value_in, value, density, sems
):
    part = lambda i: pl.ds(4 * i, 4)
    loads = [pltpu.make_async_copy(value_hbm.at[part(i)], value_in.at[part(i)], sems.at[0, i]) for i in range(4)]
    for load in loads:
        load.start()
    _, lam2, _ = first_means(row1[...])
    _, lam4, _ = second_means(row2[...], lam2)
    shift = from_row(row3[...], 0) * (1.0 / CELLS)
    scale = CELLS / from_row(row3[...], 1)
    ergodic[...] = to_row([lam4 + 2.0 * shift])
    stores = []
    for i in range(4):
        for k in range(4 * i, 4 * i + 4):
            density[k] = density_in[k] * scale[k : k + 1]
        stores.append(pltpu.make_async_copy(density.at[part(i)], density_out.at[part(i)], sems.at[1, i]))
        stores[-1].start()
    for i in range(4):
        loads[i].wait()
        for k in range(4 * i, 4 * i + 4):
            value[k] = value_in[k] - shift[k : k + 1]
        stores.append(pltpu.make_async_copy(value.at[part(i)], value_out.at[part(i)], sems.at[2, i]))
        stores[-1].start()
    for store in stores:
        store.wait()


VMEM = pl.BlockSpec(memory_space=pltpu.VMEM)
HBM = pl.BlockSpec(memory_space=pltpu.HBM)
DMA = pltpu.SemaphoreType.DMA


def kernel(body, outs, ins, scratch=(), aliases=None, vmem=16):
    call = pl.pallas_call(
        body,
        out_shape=[
            pltpu.HBM(shape[0], F32) if isinstance(shape, list) else jax.ShapeDtypeStruct(shape, F32) for shape in outs
        ],
        in_specs=ins,
        out_specs=[HBM if isinstance(shape, list) else VMEM for shape in outs],
        scratch_shapes=[pltpu.VMEM(shape, F32) if isinstance(shape, tuple) else shape for shape in scratch],
        input_output_aliases=aliases or {},
        compiler_params=pltpu.CompilerParams(vmem_limit_bytes=vmem * 1024 * 1024),
    )

    def run(*operands):
        return call(*[pltpu.with_memory_space_constraint(x, pltpu.HBM) if spec is HBM else x for x, spec in zip(operands, ins)])

    return run


def exchange(low, high, axes, count):
    before = lax.ppermute(high, axes, [(i, (i + 1) % count) for i in range(count)])
    after = lax.ppermute(low, axes, [((i + 1) % count, i) for i in range(count)])
    return before, after


def total_over_devices(row):
    rows = jnp.broadcast_to(row[None], (DEVICES, 1, 128))
    return jnp.sum(lax.all_to_all(rows, AXES, 0, 0), axis=0)


def shards(cost, density_start, coupling):
    big = (ROWS, SUB, 128)
    row = (1, 128)
    strip = (HALO + D_HALO, K, 128)
    block = (K, N, N)
    sx, dx, top, bottom, to_left, to_right = kernel(
        source_kernel,
        [big, big, strip, strip, (32, 8, 128), (32, 8, 128)],
        [HBM, HBM, HBM],
        scratch=[pltpu.SMEM((K, K), F32), block, block, DMA((2, N // CHUNK)), DMA],
    )(coupling, cost, density_start)
    above, below = exchange(top, bottom, GX, 16)
    from_left, from_right = exchange(to_left, to_right, GY, 16)
    sx, _, d_hbm, to_left, to_right, sums = kernel(
        first_sums_kernel,
        [big, big, [big], (5, 8, 128), (5, 8, 128), row],
        [VMEM] * 6,
        scratch=[DMA],
        aliases={0: 0, 1: 1},
    )(sx, dx, above, below, from_left, from_right)
    from_left, from_right = exchange(to_left, to_right, GY, 16)
    row1 = total_over_devices(sums)
    sx, w3, sums = kernel(
        second_sums_kernel, [big, [big], row], [VMEM] * 4, scratch=[big, big, big, DMA], aliases={0: 0}
    )(sx, from_left, from_right, row1)
    row2 = total_over_devices(sums)
    value, density, sums = kernel(
        last_sums_kernel,
        [[block], block, row],
        [VMEM, HBM, HBM] + [VMEM] * 4,
        scratch=[big, big, big, (ROWS, 4, SUB, 128), big, big, big, (N, K, 128), block, DMA((6,)), DMA, DMA],
        vmem=28,
    )(sx, d_hbm, w3, from_left, from_right, row1, row2)
    row3 = total_over_devices(sums)
    value, density, ergodic = kernel(
        finish_kernel,
        [[block], [block], row],
        [HBM] + [VMEM] * 4,
        scratch=[block, block, block, DMA((3, 4))],
    )(value, density, row1, row2, row3)
    return value, density, ergodic[0, :K]


def solution(mesh):
    torus = Mesh(mesh.devices.reshape(4, 2, 2, 2, 8), AXES)
    specs = (P(None, GX, GY), P(None, GX, GY), P())
    return jax.shard_map(shards, mesh=torus, in_specs=specs, out_specs=specs, check_vma=False)
```

```python
import functools

import jax
import jax.numpy as jnp
from jax import lax
from jax.experimental import pallas as pl
from jax.experimental.pallas import tpu as pltpu
from jax.sharding import Mesh
from jax.sharding import PartitionSpec as P

HALO = 10
D_HALO = 5
PAD = 4
ROW0 = PAD + HALO
N = 128
ROWS = N + 2 * ROW0
K = 16
SUB = 24
AXES = ("y", "xh", "c", "xl", "z")
GX = ("y", "xh", "c")
GY = ("xl", "z")
DEVICES = 256
CELLS = 2048.0 * 2048.0
SLOT = (0, 16, 64, 80)
BLOCK = 32
GROUPS = 4
CHUNK = 16
WAVE = 29
F32 = jnp.float32


def lanes(shape):
    return lax.broadcasted_iota(jnp.int32, shape, 1)


def roll(x, shift):
    return pltpu.roll(x, shift % 128, 1)


def between(lane, low, high):
    return (lane >= low) & (lane < high)


def recip(x):
    return 1.0 / x


def odd():
    return lax.axis_index("c") == 1, lax.axis_index("z") % 2 == 1


def pick(flag, yes, no):
    return jnp.where(jnp.broadcast_to(flag, yes.shape), yes, no)


def pack(rows, left):
    lane = lanes((8, 128))
    out = jnp.zeros((8, 128), F32)
    for (s0, s1, d0, d1), base in zip(rows, SLOT):
        for half, (s, d) in enumerate(((s0, d0), (s1, d1))):
            at = base + 32 * half
            ds = roll(s, at if left else at + HALO)
            dd = roll(d, at + HALO if left else at + HALO + D_HALO)
            out = jnp.where(between(lane, at, at + HALO), ds, out)
            out = jnp.where(between(lane, at + HALO, at + HALO + D_HALO), dd, out)
    return out


def windows(a, b):
    lane = lanes((8, 128))
    left = jnp.where(lane < 32, roll(a, 10), roll(b, 42))
    right = jnp.where(lane < 96, roll(a, 86), roll(b, 118))
    return jnp.where(lane < 64, left, right)


def halo_masks():
    lane = lanes((8, 128))
    left = between(lane, 0, 10) | between(lane, 32, 42)
    right = between(lane, 86, 96) | between(lane, 118, 128)
    return left, right


def beyond(window, from_left, from_right, i, masks, density):
    base = SLOT[i]
    a = roll(from_left, -base - 5 if density else -base)
    b = roll(from_right, 76 - base if density else 86 - base)
    return jnp.where(masks[0], a, jnp.where(masks[1], b, window))


def own(total, margin):
    lane = lanes((K, 128))
    main = jnp.where(between(lane, margin, N - margin), total[:K], 0.0)
    main = jnp.sum(main, axis=1, keepdims=True)
    if margin == 0:
        return main
    edge = total[K:]
    lane = lanes((8, 128))
    halves = []
    for half in range(2):
        at = 32 * half
        mask = between(lane, at + 10, at + 10 + margin) | between(lane, 64 + at + 22 - margin, 64 + at + 22)
        halves.append(jnp.sum(jnp.where(mask, edge, 0.0), axis=1, keepdims=True))
    return main + jnp.concatenate(halves, axis=0)


def to_row(columns):
    lane, cls = lanes((K, 128)), lax.broadcasted_iota(jnp.int32, (K, 128), 0)
    grid = jnp.zeros((K, 128), F32)
    for i, column in enumerate(columns):
        grid = jnp.where(lane == cls + K * i, column, grid)
    return jnp.sum(grid, axis=0, keepdims=True)


def from_row(row, i):
    lane, cls = lanes((K, 128)), lax.broadcasted_iota(jnp.int32, (K, 128), 0)
    return jnp.sum(jnp.where(lane == cls + K * i, row, 0.0), axis=1, keepdims=True)


def spread(column):
    wide = jnp.broadcast_to(column, (K, 128))
    lane = lanes((8, 128))
    edge = jnp.where((lane // 32) % 2 == 0, wide[:8], wide[8:])
    return jnp.concatenate([wide, edge], axis=0)


def parts(up, mid, down, s):
    left, right = roll(mid, 1), roll(mid, -1)
    px = 2.0 + jnp.abs(up - down)
    py = 2.0 + jnp.abs(left - right)
    n = s + (px * (2.0 * (up + down) + (4.0 - px)) + py * (2.0 * (left + right) + (4.0 - py)))
    return n, recip(px + py)


def row_loop(first, count, body, init=0, before=None, block=None):
    blocks = -(-count // (block or BLOCK))
    size = -(-count // blocks)
    first = first - (blocks * size - count) // 2

    def step(i, carry):
        if before is not None:
            before(i)
        return body(first + i * size, size, carry)

    return lax.fori_loop(0, blocks, step, init)


def sweep(src, s_ref, dst, lam8, minus, margin, summed=False, before=None):
    def body(r, size, total):
        rows = [src[r - 1 + i] for i in range(size + 2)]
        for i in range(size):
            n, inv = parts(rows[i], rows[i + 1], rows[i + 2], s_ref[r + i] - lam8)
            w = n * (0.25 * inv)
            if minus is not None:
                w = w - minus
            dst[r + i] = w
        return total

    row_loop(PAD + margin, ROWS - 2 * (PAD + margin), body, before=before)
    if summed:
        def add(r, size, total):
            for i in range(size):
                total = total + dst[r + i]
            return total

        return row_loop(ROW0, N, add, jnp.zeros((SUB, 128), F32))


def sweep_sums(src, s_ref, half, first=ROW0, count=N, block=None):
    def body(r, size, carry):
        a, b = carry
        rows = [src[r - 1 + i] for i in range(size + 2)]
        if half:
            rows = [row * 0.0625 + 0.5 for row in rows]
        for i in range(size):
            n, inv = parts(rows[i], rows[i + 1], rows[i + 2], s_ref[r + i])
            a = a + n * inv
            b = b + inv
        return a, b

    zero = jnp.zeros((SUB, 128), F32)
    return row_loop(first, count, body, (zero, zero), block=block)


def source_kernel(c_hbm, cost_hbm, d_hbm, sx, dx, x0, x1, y0, y1, c_ref, cost_ref, d_ref, sems, c_sem):
    odd_x, odd_y = odd()
    s2, d2 = sx.reshape(ROWS * SUB, 128), dx.reshape(ROWS * SUB, 128)
    coupling = pltpu.make_async_copy(c_hbm, c_ref, c_sem)
    coupling.start()

    def copies(i):
        part = pl.ds(pl.multiple_of(i * CHUNK, CHUNK), CHUNK)
        return (
            pltpu.make_async_copy(d_hbm.at[:, part], d_ref.at[:, part], sems.at[0, i]),
            pltpu.make_async_copy(cost_hbm.at[:, part], cost_ref.at[:, part], sems.at[1, i]),
        )

    for i in range(N // CHUNK):
        for copy in copies(i):
            copy.start()
    coupling.wait()

    def chunk(i, carry):
        for copy in copies(i):
            copy.wait()
        for part in range(CHUNK // 8):
            r = pl.multiple_of(i * CHUNK + part * 8, 8)
            dens = [d_ref[j, pl.ds(r, 8), :] for j in range(K)]
            base = (ROW0 + r) * SUB
            for j in range(K):
                d2[pl.ds(base + j, 8, stride=SUB), :] = dens[j]
            for k in range(K):
                acc = cost_ref[k, pl.ds(r, 8), :]
                for j in range(K):
                    acc = acc + c_ref[k, j] * dens[j]
                s2[pl.ds(base + k, 8, stride=SUB), :] = acc * 8.0 - 8.0
        return carry

    lax.fori_loop(0, N // CHUNK, chunk, 0)

    def group(g0, carry):
        for g in range(GROUPS):
            g = g0 * GROUPS + g
            r = ROW0 + g * 4
            rows = [(sx[r + i, 0:8], sx[r + i, 8:16], dx[r + i, 0:8], dx[r + i, 8:16]) for i in range(4)]
            left, right = pack(rows, True), pack(rows, False)
            y0[g] = pick(odd_y, left, right)
            y1[g] = pick(odd_y, right, left)
        return carry

    lax.fori_loop(0, N // 4 // GROUPS, group, 0)
    tops = [sx[ROW0 + i, 0:K] for i in range(HALO)] + [dx[ROW0 + i, 0:K] for i in range(D_HALO)]
    last = ROW0 + N
    bottoms = [sx[last - HALO + i, 0:K] for i in range(HALO)] + [dx[last - D_HALO + i, 0:K] for i in range(D_HALO)]
    for i, (top, bottom) in enumerate(zip(tops, bottoms)):
        x0[i] = pick(odd_x, top, bottom)
        x1[i] = pick(odd_x, bottom, top)


def halo_rows():
    return [(i, PAD + i) for i in range(HALO)] + [(HALO + i, ROW0 + N + i) for i in range(HALO)]


def windows_kernel(s_in, d_in, y0, y1, sx, d_hbm, sums, dx, d_sem):
    del s_in
    _, odd_y = odd()
    masks = halo_masks()

    def d_group(g0, carry):
        for g in range(GROUPS):
            g = g0 * GROUPS + g
            fl, fr = pick(odd_y, y0[g], y1[g]), pick(odd_y, y1[g], y0[g])
            for i in range(4):
                r = ROW0 + g * 4 + i
                d = d_in[r, 0:K]
                dx[r, 0:K] = d
                dx[r, K:SUB] = beyond(windows(d[:8], d[8:]), fl, fr, i, masks, True)
        return carry

    lax.fori_loop(0, N // 4 // GROUPS, d_group, 0)
    used = pl.ds(ROW0, N)
    store_d = pltpu.make_async_copy(dx.at[used], d_hbm.at[used], d_sem)
    store_d.start()

    def group(g0, total):
        for g in range(GROUPS):
            g = g0 * GROUPS + g
            fl, fr = pick(odd_y, y0[g], y1[g]), pick(odd_y, y1[g], y0[g])
            for i in range(4):
                r = ROW0 + g * 4 + i
                s = sx[r, 0:K]
                total = total + s
                sx[r, K:SUB] = beyond(windows(s[:8], s[8:]), fl, fr, i, masks, False)
        return total

    total = lax.fori_loop(0, N // 4 // GROUPS, group, jnp.zeros((K, 128), F32))
    a, b = sweep_sums(sx, sx, True, ROW0 + 1, N - 2, 42)
    sums[0, 0:K] = total
    sums[1] = a
    sums[2] = b
    store_d.wait()


def first_sums_kernel(s_in, sums_in, x0, x1, sx, d_halo, y0, y1, sums):
    del s_in
    odd_x, odd_y = odd()
    zero = jnp.zeros((8, 128), F32)
    packed = []
    for i, at in halo_rows():
        above, below = (x0, x1), (x1, x0)
        yes, no = above if i < HALO else below
        s = pick(odd_x, yes[i % HALO], no[i % HALO])
        sx[at, 0:K] = s
        sx[at, K:SUB] = windows(s[:8], s[8:])
        if HALO - D_HALO <= i < HALO + D_HALO:
            j = HALO + i % D_HALO
            d = pick(odd_x, yes[j], no[j])
            d_halo[i - (HALO - D_HALO), 0:K] = d
            d_halo[i - (HALO - D_HALO), K:SUB] = windows(d[:8], d[8:])
            packed.append((s[:8], s[8:], d[:8], d[8:]))
        else:
            packed.append((s[:8], s[8:], zero, zero))
    for g in range(5):
        rows = packed[4 * g : 4 * g + 4]
        left, right = pack(rows, True), pack(rows, False)
        y0[g] = pick(odd_y, left, right)
        y1[g] = pick(odd_y, right, left)
    a, b = sums_in[1], sums_in[2]
    for r in (ROW0, ROW0 + N - 1):
        up, mid, down = [sx[r + i] * 0.0625 + 0.5 for i in (-1, 0, 1)]
        n, inv = parts(up, mid, down, sx[r])
        a = a + n * inv
        b = b + inv
    sums[...] = to_row([jnp.sum(sums_in[0, 0:K], axis=1, keepdims=True), own(a, 1), own(b, 1)])


def first_means(row):
    lam1 = from_row(row, 0) * (0.125 / CELLS) + 1.0
    mean2 = from_row(row, 1) * (0.25 / CELLS) - lam1 * (from_row(row, 2) * (2.0 / CELLS))
    return lam1, 2.0 * mean2, mean2


def second_means(row, lam2):
    lam3 = lam2 + from_row(row, 0) * (2.0 / CELLS)
    mean4 = from_row(row, 1) * (0.25 / CELLS) - lam3 * (from_row(row, 2) * (2.0 / CELLS))
    return lam3, lam2 + 2.0 * mean4, mean4


def second_sums_kernel(s_in, y0, y1, row1, sx, w3_hbm, sums, w1, v2, w3, sem):
    del s_in
    _, odd_y = odd()
    masks = halo_masks()
    for i, at in halo_rows():
        fl, fr = pick(odd_y, y0[i // 4], y1[i // 4]), pick(odd_y, y1[i // 4], y0[i // 4])
        sx[at, K:SUB] = beyond(sx[at, K:SUB], fl, fr, i % 4, masks, False)

    def start(r, size, carry):
        for i in range(size):
            w1[r + i] = sx[r + i] * 0.0625 + 0.5
        return carry

    row_loop(PAD, ROWS - 2 * PAD, start)
    lam1, lam2, mean2 = first_means(row1[...])
    sweep(w1, sx, v2, spread(8.0 * lam1), spread(mean2), 1)
    total = sweep(v2, sx, w3, spread(8.0 * lam2), None, 2, True)
    store = pltpu.make_async_copy(w3, w3_hbm, sem)
    store.start()
    a, b = sweep_sums(w3, sx, False)
    sums[...] = to_row([own(total, 2), own(a, 3), own(b, 3)])
    store.wait()


def transpose_out(src, scratch, out):
    lane = lanes((8, 128))
    low, high = lane < 10, lane >= 118

    def body(g, carry):
        for i in range(BLOCK):
            r = g * BLOCK + i
            e = src[ROW0 + r, K:SUB]
            for half in range(2):
                a = src[ROW0 + r, 8 * half : 8 * half + 8]
                left = roll(e, -10 - 32 * half)
                right = roll(e, 42 - 32 * half)
                scratch[r, 8 * half : 8 * half + 8] = jnp.where(low, left, jnp.where(high, right, a))
        return carry

    lax.fori_loop(0, N // BLOCK, body, 0)
    flat = scratch.reshape(N * K, 128)

    def chunk(i, carry):
        for j in range(4):
            r = pl.multiple_of(i * 32 + j * 8, 8)
            for k in range(K):
                out[k, pl.ds(r, 8), :] = flat[pl.ds(r * K + k, 8, stride=K), :]
        return carry

    lax.fori_loop(0, N // 32, chunk, 0)


def weigh(w5, cs):
    def body(r, size, carry):
        rows = [w5[r - 2 + i] for i in range(size + 4)]
        for i in range(size):
            u = rows[i + 2]
            t = 4.0 + jnp.abs(rows[i + 1] - rows[i + 3]) + jnp.abs(roll(u, 1) - roll(u, -1))
            inv = recip(t)
            cs[r + i, 0] = inv + jnp.maximum(rows[i + 4] - u, 0.0) * inv
            cs[r + i, 1] = inv + jnp.maximum(rows[i] - u, 0.0) * inv
            cs[r + i, 2] = inv + jnp.maximum(roll(u, -2) - u, 0.0) * inv
            cs[r + i, 3] = inv + jnp.maximum(roll(u, 2) - u, 0.0) * inv
        return carry

    row_loop(PAD + 6, ROWS - 2 * (PAD + 6), body)


def fp(src, dst, cs, margin, summed):
    def body(r, size, total):
        rows = [src[r - 1 + i] for i in range(size + 2)]
        for i in range(size):
            u = rows[i + 1]
            fresh = (
                cs[r + i, 0] * rows[i + 2]
                + cs[r + i, 1] * rows[i]
                + cs[r + i, 2] * roll(u, -1)
                + cs[r + i, 3] * roll(u, 1)
            )
            dst[r + i] = fresh
            if summed:
                total = total + fresh
        return total

    return row_loop(PAD + margin, ROWS - 2 * (PAD + margin), body, jnp.zeros((SUB, 128), F32))


def last_sums_kernel(
    sx, d_hbm, w3_hbm, d_halo, y0, y1, row1, row2, value_hbm, density, sums,
    w3, v4, w5, cs, dx, da, db, scratch, value, w3_sems, d_sem, value_sem,
):
    size = WAVE
    first = PAD + 2
    copies = [pltpu.make_async_copy(w3_hbm.at[pl.ds(0, first + 1)], w3.at[pl.ds(0, first + 1)], w3_sems.at[5])]

    def wave(i):
        part = pl.ds(first + 1 + i * size, size)
        return pltpu.make_async_copy(w3_hbm.at[part], w3.at[part], w3_sems.at[i])

    head = copies[0]
    head.start()
    for i in range(5):
        wave(i).start()
    used = pl.ds(ROW0, N)
    load_d = pltpu.make_async_copy(d_hbm.at[used], dx.at[used], d_sem)
    load_d.start()
    _, lam2, _ = first_means(row1[...])
    lam3, lam4, mean4 = second_means(row2[...], lam2)
    head.wait()
    sweep(w3, sx, v4, spread(8.0 * lam3), spread(mean4), 3, before=lambda i: wave(i).wait())
    total5 = sweep(v4, sx, w5, spread(8.0 * lam4), None, 4, True)
    transpose_out(w5, scratch, value)
    store = pltpu.make_async_copy(value, value_hbm, value_sem)
    store.start()
    weigh(w5, cs)
    load_d.wait()
    _, odd_y = odd()
    masks = halo_masks()
    for i, at in halo_rows():
        if HALO - D_HALO <= i < HALO + D_HALO:
            fl, fr = pick(odd_y, y0[i // 4], y1[i // 4]), pick(odd_y, y1[i // 4], y0[i // 4])
            d = d_halo[i - (HALO - D_HALO)]
            dx[at, 0:K] = d[:K]
            dx[at, K:SUB] = beyond(d[K:], fl, fr, i % 4, masks, True)
    src = dx
    for n in range(5):
        dst = da if n % 2 == 0 else db
        mass = fp(src, dst, cs, 6 + n, n == 4)
        src = dst
    sums[...] = to_row([own(total5, 4), own(mass, 10)])
    transpose_out(src, scratch, density)
    store.wait()


def finish_kernel(
    value_hbm, density_in, row1, row2, row3, value_out, density_out, ergodic, value_in, value, density, sems
):
    part = lambda i: pl.ds(4 * i, 4)
    loads = [pltpu.make_async_copy(value_hbm.at[part(i)], value_in.at[part(i)], sems.at[0, i]) for i in range(4)]
    for load in loads:
        load.start()
    _, lam2, _ = first_means(row1[...])
    _, lam4, _ = second_means(row2[...], lam2)
    shift = from_row(row3[...], 0) * (1.0 / CELLS)
    scale = CELLS / from_row(row3[...], 1)
    ergodic[...] = to_row([lam4 + 2.0 * shift])
    stores = []
    for i in range(4):
        for k in range(4 * i, 4 * i + 4):
            density[k] = density_in[k] * scale[k : k + 1]
        stores.append(pltpu.make_async_copy(density.at[part(i)], density_out.at[part(i)], sems.at[1, i]))
        stores[-1].start()
    for i in range(4):
        loads[i].wait()
        for k in range(4 * i, 4 * i + 4):
            value[k] = value_in[k] - shift[k : k + 1]
        stores.append(pltpu.make_async_copy(value.at[part(i)], value_out.at[part(i)], sems.at[2, i]))
        stores[-1].start()
    for store in stores:
        store.wait()


VMEM = pl.BlockSpec(memory_space=pltpu.VMEM)
HBM = pl.BlockSpec(memory_space=pltpu.HBM)
DMA = pltpu.SemaphoreType.DMA


def kernel(body, outs, ins, scratch=(), aliases=None, vmem=16):
    call = pl.pallas_call(
        body,
        out_shape=[
            pltpu.HBM(shape[0], F32) if isinstance(shape, list) else jax.ShapeDtypeStruct(shape, F32) for shape in outs
        ],
        in_specs=ins,
        out_specs=[HBM if isinstance(shape, list) else VMEM for shape in outs],
        scratch_shapes=[pltpu.VMEM(shape, F32) if isinstance(shape, tuple) else shape for shape in scratch],
        input_output_aliases=aliases or {},
        compiler_params=pltpu.CompilerParams(vmem_limit_bytes=vmem * 1024 * 1024),
    )

    def run(*operands):
        return call(*[pltpu.with_memory_space_constraint(x, pltpu.HBM) if spec is HBM else x for x, spec in zip(operands, ins)])

    return run


def exchange(first, second, axes):
    pairs = [(i, i ^ 1) for i in range(16)], [(i, (i + 1 if i % 2 else i - 1) % 16) for i in range(16)]
    return lax.ppermute(first, axes, pairs[0]), lax.ppermute(second, axes, pairs[1])


def total_over_devices(row):
    rows = jnp.broadcast_to(row[None], (DEVICES, 1, 128))
    return jnp.sum(lax.all_to_all(rows, AXES, 0, 0), axis=0)


def shards(cost, density_start, coupling):
    big = (ROWS, SUB, 128)
    row = (1, 128)
    strip = (HALO + D_HALO, K, 128)
    block = (K, N, N)
    sx, dx, x0, x1, y0, y1 = kernel(
        source_kernel,
        [big, big, strip, strip, (32, 8, 128), (32, 8, 128)],
        [HBM, HBM, HBM],
        scratch=[pltpu.SMEM((K, K), F32), block, block, DMA((2, N // CHUNK)), DMA],
    )(coupling, cost, density_start)
    y0, y1 = exchange(y0, y1, GY)
    x0, x1 = exchange(x0, x1, GX)
    sx, d_hbm, sums = kernel(
        windows_kernel, [big, [big], (3, SUB, 128)], [VMEM] * 4, scratch=[big, DMA], aliases={0: 0}
    )(sx, dx, y0, y1)
    sx, d_halo, y0, y1, sums = kernel(
        first_sums_kernel, [big, (2 * D_HALO, SUB, 128), (5, 8, 128), (5, 8, 128), row], [VMEM] * 4, aliases={0: 0}
    )(sx, sums, x0, x1)
    y0, y1 = exchange(y0, y1, GY)
    row1 = total_over_devices(sums)
    sx, w3, sums = kernel(
        second_sums_kernel, [big, [big], row], [VMEM] * 4, scratch=[big, big, big, DMA], aliases={0: 0}
    )(sx, y0, y1, row1)
    row2 = total_over_devices(sums)
    value, density, sums = kernel(
        last_sums_kernel,
        [[block], block, row],
        [VMEM, HBM, HBM] + [VMEM] * 5,
        scratch=[big, big, big, (ROWS, 4, SUB, 128), big, big, big, (N, K, 128), block, DMA((6,)), DMA, DMA],
        vmem=28,
    )(sx, d_hbm, w3, d_halo, y0, y1, row1, row2)
    row3 = total_over_devices(sums)
    value, density, ergodic = kernel(
        finish_kernel,
        [[block], [block], row],
        [HBM] + [VMEM] * 4,
        scratch=[block, block, block, DMA((3, 4))],
    )(value, density, row1, row2, row3)
    return value, density, ergodic[0, :K]


def solution(mesh):
    torus = Mesh(mesh.devices.reshape(4, 2, 2, 2, 8), AXES)
    specs = (P(None, GX, GY), P(None, GX, GY), P())
    return jax.shard_map(shards, mesh=torus, in_specs=specs, out_specs=specs, check_vma=False)
```

```python
import functools

import jax
import jax.numpy as jnp
from jax import lax
from jax.experimental import pallas as pl
from jax.experimental.pallas import tpu as pltpu
from jax.sharding import Mesh
from jax.sharding import PartitionSpec as P

HALO = 10
D_HALO = 5
PAD = 4
ROW0 = PAD + HALO
N = 128
ROWS = N + 2 * ROW0
K = 16
SUB = 24
AXES = ("y", "xh", "c", "xl", "z")
GX = ("y", "xh", "c")
GY = ("xl", "z")
DEVICES = 256
CELLS = 2048.0 * 2048.0
SLOT = (0, 16, 64, 80)
BLOCK = 50
WEIGH = 32
FP = 72
SUMS = 64
GROUPS = 4
CHUNK = 16
WAVE = 29
F32 = jnp.float32


def lanes(shape):
    return lax.broadcasted_iota(jnp.int32, shape, 1)


def roll(x, shift):
    return pltpu.roll(x, shift % 128, 1)


def between(lane, low, high):
    return (lane >= low) & (lane < high)


def recip(x):
    return 1.0 / x


def odd():
    return lax.axis_index("c") == 1, lax.axis_index("z") % 2 == 1


def pick(flag, yes, no):
    return jnp.where(jnp.broadcast_to(flag, yes.shape), yes, no)


def pack(rows, left):
    lane = lanes((8, 128))
    out = jnp.zeros((8, 128), F32)
    for (s0, s1, d0, d1), base in zip(rows, SLOT):
        for half, (s, d) in enumerate(((s0, d0), (s1, d1))):
            at = base + 32 * half
            ds = roll(s, at if left else at + HALO)
            dd = roll(d, at + HALO if left else at + HALO + D_HALO)
            out = jnp.where(between(lane, at, at + HALO), ds, out)
            out = jnp.where(between(lane, at + HALO, at + HALO + D_HALO), dd, out)
    return out


def windows(a, b):
    lane = lanes((8, 128))
    left = jnp.where(lane < 32, roll(a, 10), roll(b, 42))
    right = jnp.where(lane < 96, roll(a, 86), roll(b, 118))
    return jnp.where(lane < 64, left, right)


def halo_masks():
    lane = lanes((8, 128))
    left = between(lane, 0, 10) | between(lane, 32, 42)
    right = between(lane, 86, 96) | between(lane, 118, 128)
    return left, right


def beyond(window, from_left, from_right, i, masks, density):
    base = SLOT[i]
    a = roll(from_left, -base - 5 if density else -base)
    b = roll(from_right, 76 - base if density else 86 - base)
    return jnp.where(masks[0], a, jnp.where(masks[1], b, window))


def own(total, margin):
    lane = lanes((K, 128))
    main = jnp.where(between(lane, margin, N - margin), total[:K], 0.0)
    main = jnp.sum(main, axis=1, keepdims=True)
    if margin == 0:
        return main
    edge = total[K:]
    lane = lanes((8, 128))
    halves = []
    for half in range(2):
        at = 32 * half
        mask = between(lane, at + 10, at + 10 + margin) | between(lane, 64 + at + 22 - margin, 64 + at + 22)
        halves.append(jnp.sum(jnp.where(mask, edge, 0.0), axis=1, keepdims=True))
    return main + jnp.concatenate(halves, axis=0)


def to_row(columns):
    lane, cls = lanes((K, 128)), lax.broadcasted_iota(jnp.int32, (K, 128), 0)
    grid = jnp.zeros((K, 128), F32)
    for i, column in enumerate(columns):
        grid = jnp.where(lane == cls + K * i, column, grid)
    return jnp.sum(grid, axis=0, keepdims=True)


def from_row(row, i):
    lane, cls = lanes((K, 128)), lax.broadcasted_iota(jnp.int32, (K, 128), 0)
    return jnp.sum(jnp.where(lane == cls + K * i, row, 0.0), axis=1, keepdims=True)


def spread(column):
    wide = jnp.broadcast_to(column, (K, 128))
    lane = lanes((8, 128))
    edge = jnp.where((lane // 32) % 2 == 0, wide[:8], wide[8:])
    return jnp.concatenate([wide, edge], axis=0)


def parts(up, mid, down, s):
    left, right = roll(mid, 1), roll(mid, -1)
    px = 2.0 + jnp.abs(up - down)
    py = 2.0 + jnp.abs(left - right)
    n = s + (px * (2.0 * (up + down) + (4.0 - px)) + py * (2.0 * (left + right) + (4.0 - py)))
    return n, recip(px + py)


def row_loop(first, count, body, init=0, before=None, block=None):
    blocks = -(-count // (block or BLOCK))
    size = -(-count // blocks)
    first = first - (blocks * size - count) // 2

    def step(i, carry):
        if before is not None:
            before(i)
        return body(first + i * size, size, carry)

    return lax.fori_loop(0, blocks, step, init)


def sweep(src, s_ref, dst, lam8, minus, margin, summed=False, before=None, half=False):
    def body(r, size, total):
        rows = [src[r - 1 + i] for i in range(size + 2)]
        if half:
            rows = [row * 0.0625 + 0.5 for row in rows]
        for i in range(size):
            n, inv = parts(rows[i], rows[i + 1], rows[i + 2], s_ref[r + i] - lam8)
            w = n * (0.25 * inv)
            if minus is not None:
                w = w - minus
            dst[r + i] = w
        return total

    row_loop(PAD + margin, ROWS - 2 * (PAD + margin), body, before=before, block=32 if before else None)
    if summed:
        def add(r, size, total):
            for i in range(size):
                total = total + dst[r + i]
            return total

        return row_loop(ROW0, N, add, jnp.zeros((SUB, 128), F32), block=SUMS)


def sweep_sums(src, s_ref, half):
    def body(r, size, carry):
        a, b = carry
        rows = [src[r - 1 + i] for i in range(size + 2)]
        if half:
            rows = [row * 0.0625 + 0.5 for row in rows]
        for i in range(size):
            n, inv = parts(rows[i], rows[i + 1], rows[i + 2], s_ref[r + i])
            a = a + n * inv
            b = b + inv
        return a, b

    zero = jnp.zeros((SUB, 128), F32)
    return row_loop(ROW0, N, body, (zero, zero), block=SUMS)


def source_kernel(c_hbm, cost_hbm, d_hbm, sx, dx, x0, x1, y0, y1, c_ref, cost_ref, d_ref, sems, c_sem):
    odd_x, odd_y = odd()
    s2, d2 = sx.reshape(ROWS * SUB, 128), dx.reshape(ROWS * SUB, 128)
    coupling = pltpu.make_async_copy(c_hbm, c_ref, c_sem)
    coupling.start()

    def copies(i):
        part = pl.ds(pl.multiple_of(i * CHUNK, CHUNK), CHUNK)
        return (
            pltpu.make_async_copy(d_hbm.at[:, part], d_ref.at[:, part], sems.at[0, i]),
            pltpu.make_async_copy(cost_hbm.at[:, part], cost_ref.at[:, part], sems.at[1, i]),
        )

    for i in range(N // CHUNK):
        for copy in copies(i):
            copy.start()
    coupling.wait()

    def chunk(i, carry):
        for copy in copies(i):
            copy.wait()
        for part in range(CHUNK // 8):
            r = pl.multiple_of(i * CHUNK + part * 8, 8)
            dens = [d_ref[j, pl.ds(r, 8), :] for j in range(K)]
            base = (ROW0 + r) * SUB
            for j in range(K):
                d2[pl.ds(base + j, 8, stride=SUB), :] = dens[j]
            for k in range(K):
                acc = cost_ref[k, pl.ds(r, 8), :]
                for j in range(K):
                    acc = acc + c_ref[k, j] * dens[j]
                s2[pl.ds(base + k, 8, stride=SUB), :] = acc * 8.0 - 8.0
        return carry

    lax.fori_loop(0, N // CHUNK, chunk, 0)

    def group(g0, carry):
        for g in range(GROUPS):
            g = g0 * GROUPS + g
            r = ROW0 + g * 4
            rows = [(sx[r + i, 0:8], sx[r + i, 8:16], dx[r + i, 0:8], dx[r + i, 8:16]) for i in range(4)]
            left, right = pack(rows, True), pack(rows, False)
            y0[g] = pick(odd_y, left, right)
            y1[g] = pick(odd_y, right, left)
        return carry

    lax.fori_loop(0, N // 4 // GROUPS, group, 0)
    tops = [sx[ROW0 + i, 0:K] for i in range(HALO)] + [dx[ROW0 + i, 0:K] for i in range(D_HALO)]
    last = ROW0 + N
    bottoms = [sx[last - HALO + i, 0:K] for i in range(HALO)] + [dx[last - D_HALO + i, 0:K] for i in range(D_HALO)]
    for i, (top, bottom) in enumerate(zip(tops, bottoms)):
        x0[i] = pick(odd_x, top, bottom)
        x1[i] = pick(odd_x, bottom, top)


def halo_rows():
    return [(i, PAD + i) for i in range(HALO)] + [(HALO + i, ROW0 + N + i) for i in range(HALO)]


def halo_rows_kernel(s_in, x0, x1, sx, d_halo, y0, y1):
    del s_in
    odd_x, odd_y = odd()
    zero = jnp.zeros((8, 128), F32)
    packed = []
    for i, at in halo_rows():
        above, below = (x0, x1), (x1, x0)
        yes, no = above if i < HALO else below
        s = pick(odd_x, yes[i % HALO], no[i % HALO])
        sx[at, 0:K] = s
        sx[at, K:SUB] = windows(s[:8], s[8:])
        if HALO - D_HALO <= i < HALO + D_HALO:
            j = HALO + i % D_HALO
            d = pick(odd_x, yes[j], no[j])
            d_halo[i - (HALO - D_HALO), 0:K] = d
            d_halo[i - (HALO - D_HALO), K:SUB] = windows(d[:8], d[8:])
            packed.append((s[:8], s[8:], d[:8], d[8:]))
        else:
            packed.append((s[:8], s[8:], zero, zero))
    for g in range(5):
        rows = packed[4 * g : 4 * g + 4]
        left, right = pack(rows, True), pack(rows, False)
        y0[g] = pick(odd_y, left, right)
        y1[g] = pick(odd_y, right, left)


def first_sums_kernel(s_in, d_in, y0, y1, sx, d_hbm, sums, dx, d_sem):
    del s_in
    _, odd_y = odd()
    masks = halo_masks()

    def d_group(g0, carry):
        for g in range(GROUPS):
            g = g0 * GROUPS + g
            fl, fr = pick(odd_y, y0[g], y1[g]), pick(odd_y, y1[g], y0[g])
            for i in range(4):
                r = ROW0 + g * 4 + i
                d = d_in[r, 0:K]
                dx[r, 0:K] = d
                dx[r, K:SUB] = beyond(windows(d[:8], d[8:]), fl, fr, i, masks, True)
        return carry

    lax.fori_loop(0, N // 4 // GROUPS, d_group, 0)
    used = pl.ds(ROW0, N)
    store_d = pltpu.make_async_copy(dx.at[used], d_hbm.at[used], d_sem)
    store_d.start()

    def group(g0, total):
        for g in range(GROUPS):
            g = g0 * GROUPS + g
            fl, fr = pick(odd_y, y0[g], y1[g]), pick(odd_y, y1[g], y0[g])
            for i in range(4):
                r = ROW0 + g * 4 + i
                s = sx[r, 0:K]
                total = total + s
                sx[r, K:SUB] = beyond(windows(s[:8], s[8:]), fl, fr, i, masks, False)
        return total

    total = lax.fori_loop(0, N // 4 // GROUPS, group, jnp.zeros((K, 128), F32))
    a, b = sweep_sums(sx, sx, True)
    sums[...] = to_row([jnp.sum(total, axis=1, keepdims=True), own(a, 1), own(b, 1)])
    store_d.wait()


def first_means(row):
    lam1 = from_row(row, 0) * (0.125 / CELLS) + 1.0
    mean2 = from_row(row, 1) * (0.25 / CELLS) - lam1 * (from_row(row, 2) * (2.0 / CELLS))
    return lam1, 2.0 * mean2, mean2


def second_means(row, lam2):
    lam3 = lam2 + from_row(row, 0) * (2.0 / CELLS)
    mean4 = from_row(row, 1) * (0.25 / CELLS) - lam3 * (from_row(row, 2) * (2.0 / CELLS))
    return lam3, lam2 + 2.0 * mean4, mean4


def second_sums_kernel(s_in, y0, y1, row1, sx, w3_hbm, sums, v2, w3, sem):
    del s_in
    _, odd_y = odd()
    masks = halo_masks()
    for i, at in halo_rows():
        fl, fr = pick(odd_y, y0[i // 4], y1[i // 4]), pick(odd_y, y1[i // 4], y0[i // 4])
        sx[at, K:SUB] = beyond(sx[at, K:SUB], fl, fr, i % 4, masks, False)

    lam1, lam2, mean2 = first_means(row1[...])
    sweep(sx, sx, v2, spread(8.0 * lam1), spread(mean2), 1, half=True)
    total = sweep(v2, sx, w3, spread(8.0 * lam2), None, 2, True)
    store = pltpu.make_async_copy(w3, w3_hbm, sem)
    store.start()
    a, b = sweep_sums(w3, sx, False)
    sums[...] = to_row([own(total, 2), own(a, 3), own(b, 3)])
    store.wait()


def transpose_out(src, out):
    lane = lanes((8, 128))
    low, high = lane < 10, lane >= 118
    flat = out.reshape(K * N, 128)

    def body(g, carry):
        for i in range(32):
            r = g * 32 + i
            e = src[ROW0 + r, K:SUB]
            for half in range(2):
                a = src[ROW0 + r, 8 * half : 8 * half + 8]
                left = roll(e, -10 - 32 * half)
                right = roll(e, 42 - 32 * half)
                flat[pl.ds(8 * half * N + r, 8, stride=N), :] = jnp.where(low, left, jnp.where(high, right, a))
        return carry

    lax.fori_loop(0, N // 32, body, 0)


def weigh(w5, d, cs, inv_ref, s0):
    def body(r, size, carry):
        rows = [w5[r - 1 + i] for i in range(size + 2)]
        for i in range(size):
            u = rows[i + 1]
            dx, dy = rows[i] - rows[i + 2], roll(u, 1) - roll(u, -1)
            xp, yp = jnp.maximum(dx, 0.0), jnp.maximum(dy, 0.0)
            xm, ym = xp - dx, yp - dy
            t = 4.0 + ((xp + xm) + (yp + ym))
            inv = recip(t)
            inv_ref[r + i] = inv
            s0[r + i] = d[r + i] * t
            for n, p in enumerate((xp, xm, yp, ym)):
                cs[r + i, n] = inv + p * inv
        return carry

    row_loop(PAD + 5, ROWS - 2 * (PAD + 5), body, block=WEIGH)


def fp(src, dst, cs, margin, inv_ref=None):
    def body(r, size, total):
        rows = [src[r - 1 + i] for i in range(size + 2)]
        for i in range(size):
            u = rows[i + 1]
            along_x = cs[r + i - 1, 0] * rows[i] + cs[r + i + 1, 1] * rows[i + 2]
            along_y = roll(cs[r + i, 2] * u, 1) + roll(cs[r + i, 3] * u, -1)
            fresh = along_x + along_y
            if inv_ref is not None:
                fresh = fresh * inv_ref[r + i]
                total = total + fresh
            dst[r + i] = fresh
        return total

    return row_loop(PAD + margin, ROWS - 2 * (PAD + margin), body, jnp.zeros((SUB, 128), F32), block=FP)


def last_sums_kernel(
    sx, d_hbm, w3_hbm, d_halo, y0, y1, row1, row2, value_hbm, density, sums, lam4_row,
    w3, v4, w5, cs, dx, da, db, inv, value, w3_sems, d_sem, value_sem,
):
    size = WAVE
    first = PAD + 2
    copies = [pltpu.make_async_copy(w3_hbm.at[pl.ds(0, first + 1)], w3.at[pl.ds(0, first + 1)], w3_sems.at[5])]

    def wave(i):
        part = pl.ds(first + 1 + i * size, size)
        return pltpu.make_async_copy(w3_hbm.at[part], w3.at[part], w3_sems.at[i])

    head = copies[0]
    head.start()
    for i in range(5):
        wave(i).start()
    used = pl.ds(ROW0, N)
    load_d = pltpu.make_async_copy(d_hbm.at[used], dx.at[used], d_sem)
    load_d.start()
    _, lam2, _ = first_means(row1[...])
    lam3, lam4, mean4 = second_means(row2[...], lam2)
    lam4_row[...] = to_row([lam4])
    head.wait()
    sweep(w3, sx, v4, spread(8.0 * lam3), spread(mean4), 3, before=lambda i: wave(i).wait())
    total5 = sweep(v4, sx, w5, spread(8.0 * lam4), None, 4, True)
    transpose_out(w5, value)
    store = pltpu.make_async_copy(value, value_hbm, value_sem)
    store.start()
    load_d.wait()
    _, odd_y = odd()
    masks = halo_masks()
    for i, at in halo_rows():
        if HALO - D_HALO <= i < HALO + D_HALO:
            fl, fr = pick(odd_y, y0[i // 4], y1[i // 4]), pick(odd_y, y1[i // 4], y0[i // 4])
            d = d_halo[i - (HALO - D_HALO)]
            dx[at, 0:K] = d[:K]
            dx[at, K:SUB] = beyond(d[K:], fl, fr, i % 4, masks, True)
    weigh(w5, dx, cs, inv, db)
    src, other = db, da
    for n in range(5):
        mass = fp(src, other, cs, 6 + n, inv if n == 4 else None)
        src, other = other, src
    sums[...] = to_row([own(total5, 4), own(mass, 10)])
    transpose_out(src, density)
    store.wait()


def finish_kernel(
    value_hbm, density_in, lam4_row, row3, value_out, density_out, ergodic, value_in, value, density, sems
):
    part = lambda i: pl.ds(4 * i, 4)
    loads = [pltpu.make_async_copy(value_hbm.at[part(i)], value_in.at[part(i)], sems.at[0, i]) for i in range(4)]
    for load in loads:
        load.start()
    shift = from_row(row3[...], 0) * (1.0 / CELLS)
    scale = CELLS / from_row(row3[...], 1)
    ergodic[...] = (lam4_row[...] + row3[...] * (2.0 / CELLS))[0, :K]
    stores = []
    for i in range(4):
        for k in range(4 * i, 4 * i + 4):
            density[k] = density_in[k] * scale[k : k + 1]
        stores.append(pltpu.make_async_copy(density.at[part(i)], density_out.at[part(i)], sems.at[1, i]))
        stores[-1].start()
    for i in range(4):
        loads[i].wait()
        for k in range(4 * i, 4 * i + 4):
            value[k] = value_in[k] - shift[k : k + 1]
        stores.append(pltpu.make_async_copy(value.at[part(i)], value_out.at[part(i)], sems.at[2, i]))
        stores[-1].start()
    for store in stores:
        store.wait()


VMEM = pl.BlockSpec(memory_space=pltpu.VMEM)
HBM = pl.BlockSpec(memory_space=pltpu.HBM)
DMA = pltpu.SemaphoreType.DMA


def kernel(body, outs, ins, scratch=(), aliases=None, vmem=16):
    call = pl.pallas_call(
        body,
        out_shape=[
            pltpu.HBM(shape[0], F32) if isinstance(shape, list) else jax.ShapeDtypeStruct(shape, F32) for shape in outs
        ],
        in_specs=ins,
        out_specs=[HBM if isinstance(shape, list) else VMEM for shape in outs],
        scratch_shapes=[pltpu.VMEM(shape, F32) if isinstance(shape, tuple) else shape for shape in scratch],
        input_output_aliases=aliases or {},
        compiler_params=pltpu.CompilerParams(vmem_limit_bytes=vmem * 1024 * 1024),
    )

    def run(*operands):
        return call(*[pltpu.with_memory_space_constraint(x, pltpu.HBM) if spec is HBM else x for x, spec in zip(operands, ins)])

    return run


def exchange(first, second, axes):
    pairs = [(i, i ^ 1) for i in range(16)], [(i, (i + 1 if i % 2 else i - 1) % 16) for i in range(16)]
    return lax.ppermute(first, axes, pairs[0]), lax.ppermute(second, axes, pairs[1])


def total_over_devices(row):
    rows = jnp.broadcast_to(row[None], (DEVICES, 1, 128))
    return jnp.sum(lax.all_to_all(rows, AXES, 0, 0), axis=0)


def shards(cost, density_start, coupling):
    big = (ROWS, SUB, 128)
    row = (1, 128)
    strip = (HALO + D_HALO, K, 128)
    block = (K, N, N)
    sx, dx, x0, x1, y0, y1 = kernel(
        source_kernel,
        [big, big, strip, strip, (32, 8, 128), (32, 8, 128)],
        [HBM, HBM, HBM],
        scratch=[pltpu.SMEM((K, K), F32), block, block, DMA((2, N // CHUNK)), DMA],
    )(coupling, cost, density_start)
    x0, x1 = exchange(x0, x1, GX)
    y0, y1 = exchange(y0, y1, GY)
    sx, d_halo, z0, z1 = kernel(
        halo_rows_kernel, [big, (2 * D_HALO, SUB, 128), (5, 8, 128), (5, 8, 128)], [VMEM] * 3, aliases={0: 0}
    )(sx, x0, x1)
    z0, z1 = exchange(z0, z1, GY)
    sx, d_hbm, sums = kernel(
        first_sums_kernel, [big, [big], row], [VMEM] * 4, scratch=[big, DMA], aliases={0: 0}
    )(sx, dx, y0, y1)
    sums, y0, y1 = lax.optimization_barrier((sums, z0, z1))
    row1 = total_over_devices(sums)
    sx, w3, sums = kernel(
        second_sums_kernel, [big, [big], row], [VMEM] * 4, scratch=[big, big, DMA], aliases={0: 0}
    )(sx, y0, y1, row1)
    row2 = total_over_devices(sums)
    value, density, sums, lam4 = kernel(
        last_sums_kernel,
        [[block], block, row, row],
        [VMEM, HBM, HBM] + [VMEM] * 5,
        scratch=[big, big, big, (ROWS, 4, SUB, 128), big, big, big, big, block, DMA((6,)), DMA, DMA],
        vmem=28,
    )(sx, d_hbm, w3, d_halo, y0, y1, row1, row2)
    row3 = total_over_devices(sums)
    value, density, ergodic = kernel(
        finish_kernel,
        [[block], [block], (K,)],
        [HBM] + [VMEM] * 3,
        scratch=[block, block, block, DMA((3, 4))],
    )(value, density, lam4, row3)
    return value, density, ergodic


def solution(mesh):
    torus = Mesh(mesh.devices.reshape(4, 2, 2, 2, 8), AXES)
    specs = (P(None, GX, GY), P(None, GX, GY), P())
    return jax.shard_map(shards, mesh=torus, in_specs=specs, out_specs=specs, check_vma=False)
```

```python
import functools

import jax
import jax.numpy as jnp
from jax import lax
from jax.experimental import pallas as pl
from jax.experimental.pallas import tpu as pltpu
from jax.sharding import Mesh
from jax.sharding import PartitionSpec as P

HALO = 10
D_HALO = 5
PAD = 4
ROW0 = PAD + HALO
N = 128
ROWS = N + 2 * ROW0
K = 16
SUB = 24
AXES = ("y", "xh", "c", "xl", "z")
GX = ("y", "xh", "c")
GY = ("xl", "z")
DEVICES = 256
CELLS = 2048.0 * 2048.0
SLOT = (0, 16, 64, 80)
BLOCK = 50
WEIGH = 32
FP = 72
SUMS = 64
GROUPS = 4
CHUNK = 16
WAVE = 29
F32 = jnp.float32


def lanes(shape):
    return lax.broadcasted_iota(jnp.int32, shape, 1)


def roll(x, shift):
    return pltpu.roll(x, shift % 128, 1)


def between(lane, low, high):
    return (lane >= low) & (lane < high)


def recip(x):
    return 1.0 / x


def odd():
    return lax.axis_index("c") == 1, lax.axis_index("z") % 2 == 1


def pick(flag, yes, no):
    return jnp.where(jnp.broadcast_to(flag, yes.shape), yes, no)


def pack(rows, left):
    lane = lanes((8, 128))
    out = jnp.zeros((8, 128), F32)
    for (s0, s1, d0, d1), base in zip(rows, SLOT):
        for half, (s, d) in enumerate(((s0, d0), (s1, d1))):
            at = base + 32 * half
            ds = roll(s, at if left else at + HALO)
            dd = roll(d, at + HALO if left else at + HALO + D_HALO)
            out = jnp.where(between(lane, at, at + HALO), ds, out)
            out = jnp.where(between(lane, at + HALO, at + HALO + D_HALO), dd, out)
    return out


def windows(a, b):
    lane = lanes((8, 128))
    left = jnp.where(lane < 32, roll(a, 10), roll(b, 42))
    right = jnp.where(lane < 96, roll(a, 86), roll(b, 118))
    return jnp.where(lane < 64, left, right)


def halo_masks():
    lane = lanes((8, 128))
    left = between(lane, 0, 10) | between(lane, 32, 42)
    right = between(lane, 86, 96) | between(lane, 118, 128)
    return left, right


def beyond(window, from_left, from_right, i, masks, density):
    base = SLOT[i]
    a = roll(from_left, -base - 5 if density else -base)
    b = roll(from_right, 76 - base if density else 86 - base)
    return jnp.where(masks[0], a, jnp.where(masks[1], b, window))


def own(total, margin):
    lane = lanes((K, 128))
    main = jnp.where(between(lane, margin, N - margin), total[:K], 0.0)
    main = jnp.sum(main, axis=1, keepdims=True)
    if margin == 0:
        return main
    edge = total[K:]
    lane = lanes((8, 128))
    halves = []
    for half in range(2):
        at = 32 * half
        mask = between(lane, at + 10, at + 10 + margin) | between(lane, 64 + at + 22 - margin, 64 + at + 22)
        halves.append(jnp.sum(jnp.where(mask, edge, 0.0), axis=1, keepdims=True))
    return main + jnp.concatenate(halves, axis=0)


def to_row(columns):
    lane, cls = lanes((K, 128)), lax.broadcasted_iota(jnp.int32, (K, 128), 0)
    grid = jnp.zeros((K, 128), F32)
    for i, column in enumerate(columns):
        grid = jnp.where(lane == cls + K * i, column, grid)
    return jnp.sum(grid, axis=0, keepdims=True)


def from_row(row, i):
    lane, cls = lanes((K, 128)), lax.broadcasted_iota(jnp.int32, (K, 128), 0)
    return jnp.sum(jnp.where(lane == cls + K * i, row, 0.0), axis=1, keepdims=True)


def spread(column):
    wide = jnp.broadcast_to(column, (K, 128))
    lane = lanes((8, 128))
    edge = jnp.where((lane // 32) % 2 == 0, wide[:8], wide[8:])
    return jnp.concatenate([wide, edge], axis=0)


def parts(up, mid, down, s):
    left, right = roll(mid, 1), roll(mid, -1)
    px = 2.0 + jnp.abs(up - down)
    py = 2.0 + jnp.abs(left - right)
    n = s + (px * (2.0 * (up + down) + (4.0 - px)) + py * (2.0 * (left + right) + (4.0 - py)))
    return n, recip(px + py)


def row_loop(first, count, body, init=0, before=None, block=None):
    blocks = -(-count // (block or BLOCK))
    size = -(-count // blocks)
    first = first - (blocks * size - count) // 2

    def step(i, carry):
        if before is not None:
            before(i)
        return body(first + i * size, size, carry)

    return lax.fori_loop(0, blocks, step, init)


def sweep(src, s_ref, dst, lam8, minus, margin, summed=False, before=None, half=False):
    def body(r, size, total):
        rows = [src[r - 1 + i] for i in range(size + 2)]
        if half:
            rows = [row * 0.0625 + 0.5 for row in rows]
        for i in range(size):
            n, inv = parts(rows[i], rows[i + 1], rows[i + 2], s_ref[r + i] - lam8)
            w = n * (0.25 * inv)
            if minus is not None:
                w = w - minus
            dst[r + i] = w
        return total

    row_loop(PAD + margin, ROWS - 2 * (PAD + margin), body, before=before, block=32 if before else None)
    if summed:
        def add(r, size, total):
            for i in range(size):
                total = total + dst[r + i]
            return total

        return row_loop(ROW0, N, add, jnp.zeros((SUB, 128), F32), block=SUMS)


def sweep_sums(src, s_ref, half, first=ROW0, count=N):
    def body(r, size, carry):
        a, b = carry
        rows = [src[r - 1 + i] for i in range(size + 2)]
        if half:
            rows = [row * 0.0625 + 0.5 for row in rows]
        for i in range(size):
            n, inv = parts(rows[i], rows[i + 1], rows[i + 2], s_ref[r + i])
            a = a + n * inv
            b = b + inv
        return a, b

    zero = jnp.zeros((SUB, 128), F32)
    return row_loop(first, count, body, (zero, zero), block=count // 2)


def source_kernel(c_hbm, cost_hbm, d_hbm, sx, dx, x0, x1, y0, y1, c_ref, cost_ref, d_ref, sems, c_sem):
    odd_x, odd_y = odd()
    s2, d2 = sx.reshape(ROWS * SUB, 128), dx.reshape(ROWS * SUB, 128)
    coupling = pltpu.make_async_copy(c_hbm, c_ref, c_sem)
    coupling.start()

    def copies(i):
        part = pl.ds(pl.multiple_of(i * CHUNK, CHUNK), CHUNK)
        return (
            pltpu.make_async_copy(d_hbm.at[:, part], d_ref.at[:, part], sems.at[0, i]),
            pltpu.make_async_copy(cost_hbm.at[:, part], cost_ref.at[:, part], sems.at[1, i]),
        )

    for i in range(N // CHUNK):
        for copy in copies(i):
            copy.start()
    coupling.wait()

    def chunk(i, carry):
        for copy in copies(i):
            copy.wait()
        for part in range(CHUNK // 8):
            r = pl.multiple_of(i * CHUNK + part * 8, 8)
            dens = [d_ref[j, pl.ds(r, 8), :] for j in range(K)]
            base = (ROW0 + r) * SUB
            for j in range(K):
                d2[pl.ds(base + j, 8, stride=SUB), :] = dens[j]
            for k in range(K):
                acc = cost_ref[k, pl.ds(r, 8), :]
                for j in range(K):
                    acc = acc + c_ref[k, j] * dens[j]
                s2[pl.ds(base + k, 8, stride=SUB), :] = acc * 8.0 - 8.0
        for g in range(CHUNK // 4):
            g = i * (CHUNK // 4) + g
            r = ROW0 + g * 4
            rows = [(sx[r + i, 0:8], sx[r + i, 8:16], dx[r + i, 0:8], dx[r + i, 8:16]) for i in range(4)]
            left, right = pack(rows, True), pack(rows, False)
            y0[g] = pick(odd_y, left, right)
            y1[g] = pick(odd_y, right, left)
        return carry

    lax.fori_loop(0, N // CHUNK, chunk, 0)

    tops = [sx[ROW0 + i, 0:K] for i in range(HALO)] + [dx[ROW0 + i, 0:K] for i in range(D_HALO)]
    last = ROW0 + N
    bottoms = [sx[last - HALO + i, 0:K] for i in range(HALO)] + [dx[last - D_HALO + i, 0:K] for i in range(D_HALO)]
    for i, (top, bottom) in enumerate(zip(tops, bottoms)):
        x0[i] = pick(odd_x, top, bottom)
        x1[i] = pick(odd_x, bottom, top)


def halo_rows():
    return [(i, PAD + i) for i in range(HALO)] + [(HALO + i, ROW0 + N + i) for i in range(HALO)]


def windows_kernel(s_in, d_in, y0, y1, sx, d_hbm, sums, dx, d_sem):
    del s_in
    _, odd_y = odd()
    masks = halo_masks()

    def d_group(g0, carry):
        for g in range(GROUPS):
            g = g0 * GROUPS + g
            fl, fr = pick(odd_y, y0[g], y1[g]), pick(odd_y, y1[g], y0[g])
            for i in range(4):
                r = ROW0 + g * 4 + i
                d = d_in[r, 0:K]
                dx[r, 0:K] = d
                dx[r, K:SUB] = beyond(windows(d[:8], d[8:]), fl, fr, i, masks, True)
        return carry

    lax.fori_loop(0, N // 4 // GROUPS, d_group, 0)
    used = pl.ds(ROW0, N)
    store_d = pltpu.make_async_copy(dx.at[used], d_hbm.at[used], d_sem)
    store_d.start()

    def group(g0, total):
        for g in range(GROUPS):
            g = g0 * GROUPS + g
            fl, fr = pick(odd_y, y0[g], y1[g]), pick(odd_y, y1[g], y0[g])
            for i in range(4):
                r = ROW0 + g * 4 + i
                s = sx[r, 0:K]
                total = total + s
                sx[r, K:SUB] = beyond(windows(s[:8], s[8:]), fl, fr, i, masks, False)
        return total

    total = lax.fori_loop(0, N // 4 // GROUPS, group, jnp.zeros((K, 128), F32))
    a, b = sweep_sums(sx, sx, True, ROW0 + 1, N - 2)
    sums[0, 0:K] = total
    sums[1] = a
    sums[2] = b
    store_d.wait()


def first_sums_kernel(s_in, sums_in, x0, x1, sx, d_halo, y0, y1, sums):
    del s_in
    odd_x, odd_y = odd()
    zero = jnp.zeros((8, 128), F32)
    packed = []
    for i, at in halo_rows():
        above, below = (x0, x1), (x1, x0)
        yes, no = above if i < HALO else below
        s = pick(odd_x, yes[i % HALO], no[i % HALO])
        sx[at, 0:K] = s
        sx[at, K:SUB] = windows(s[:8], s[8:])
        if HALO - D_HALO <= i < HALO + D_HALO:
            j = HALO + i % D_HALO
            d = pick(odd_x, yes[j], no[j])
            d_halo[i - (HALO - D_HALO), 0:K] = d
            d_halo[i - (HALO - D_HALO), K:SUB] = windows(d[:8], d[8:])
            packed.append((s[:8], s[8:], d[:8], d[8:]))
        else:
            packed.append((s[:8], s[8:], zero, zero))
    for g in range(5):
        rows = packed[4 * g : 4 * g + 4]
        left, right = pack(rows, True), pack(rows, False)
        y0[g] = pick(odd_y, left, right)
        y1[g] = pick(odd_y, right, left)
    a, b = sums_in[1], sums_in[2]
    for r in (ROW0, ROW0 + N - 1):
        up, mid, down = [sx[r + i] * 0.0625 + 0.5 for i in (-1, 0, 1)]
        n, inv = parts(up, mid, down, sx[r])
        a = a + n * inv
        b = b + inv
    sums[...] = to_row([jnp.sum(sums_in[0, 0:K], axis=1, keepdims=True), own(a, 1), own(b, 1)])


def first_means(row):
    lam1 = from_row(row, 0) * (0.125 / CELLS) + 1.0
    mean2 = from_row(row, 1) * (0.25 / CELLS) - lam1 * (from_row(row, 2) * (2.0 / CELLS))
    return lam1, 2.0 * mean2, mean2


def second_means(row, lam2):
    lam3 = lam2 + from_row(row, 0) * (2.0 / CELLS)
    mean4 = from_row(row, 1) * (0.25 / CELLS) - lam3 * (from_row(row, 2) * (2.0 / CELLS))
    return lam3, lam2 + 2.0 * mean4, mean4


def second_sums_kernel(s_in, y0, y1, row1, sx, w3_hbm, sums, v2, w3, sem):
    del s_in
    _, odd_y = odd()
    masks = halo_masks()
    for i, at in halo_rows():
        fl, fr = pick(odd_y, y0[i // 4], y1[i // 4]), pick(odd_y, y1[i // 4], y0[i // 4])
        sx[at, K:SUB] = beyond(sx[at, K:SUB], fl, fr, i % 4, masks, False)

    lam1, lam2, mean2 = first_means(row1[...])
    sweep(sx, sx, v2, spread(8.0 * lam1), spread(mean2), 1, half=True)
    total = sweep(v2, sx, w3, spread(8.0 * lam2), None, 2, True)
    store = pltpu.make_async_copy(w3, w3_hbm, sem)
    store.start()
    a, b = sweep_sums(w3, sx, False)
    sums[...] = to_row([own(total, 2), own(a, 3), own(b, 3)])
    store.wait()


def transpose_out(src, out):
    lane = lanes((8, 128))
    low, high = lane < 10, lane >= 118
    flat = out.reshape(K * N, 128)

    def body(g, carry):
        for i in range(32):
            r = g * 32 + i
            e = src[ROW0 + r, K:SUB]
            for half in range(2):
                a = src[ROW0 + r, 8 * half : 8 * half + 8]
                left = roll(e, -10 - 32 * half)
                right = roll(e, 42 - 32 * half)
                flat[pl.ds(8 * half * N + r, 8, stride=N), :] = jnp.where(low, left, jnp.where(high, right, a))
        return carry

    lax.fori_loop(0, N // 32, body, 0)


def weigh(w5, d, cs, inv_ref, s0):
    def body(r, size, carry):
        rows = [w5[r - 1 + i] for i in range(size + 2)]
        for i in range(size):
            u = rows[i + 1]
            dx, dy = rows[i] - rows[i + 2], roll(u, 1) - roll(u, -1)
            xp, yp = jnp.maximum(dx, 0.0), jnp.maximum(dy, 0.0)
            xm, ym = xp - dx, yp - dy
            t = 4.0 + ((xp + xm) + (yp + ym))
            inv = recip(t)
            inv_ref[r + i] = inv
            s0[r + i] = d[r + i] * t
            for n, p in enumerate((xp, xm, yp, ym)):
                cs[r + i, n] = inv + p * inv
        return carry

    row_loop(PAD + 5, ROWS - 2 * (PAD + 5), body, block=WEIGH)


def fp(src, dst, cs, margin, inv_ref=None):
    def body(r, size, total):
        rows = [src[r - 1 + i] for i in range(size + 2)]
        for i in range(size):
            u = rows[i + 1]
            along_x = cs[r + i - 1, 0] * rows[i] + cs[r + i + 1, 1] * rows[i + 2]
            along_y = roll(cs[r + i, 2] * u, 1) + roll(cs[r + i, 3] * u, -1)
            fresh = along_x + along_y
            if inv_ref is not None:
                fresh = fresh * inv_ref[r + i]
                total = total + fresh
            dst[r + i] = fresh
        return total

    return row_loop(PAD + margin, ROWS - 2 * (PAD + margin), body, jnp.zeros((SUB, 128), F32), block=FP)


def last_sums_kernel(
    sx, d_hbm, w3_hbm, d_halo, y0, y1, row1, row2, value_hbm, density, sums, lam4_row,
    w3, v4, w5, cs, dx, da, db, inv, value, w3_sems, d_sem, value_sem,
):
    size = WAVE
    first = PAD + 2
    copies = [pltpu.make_async_copy(w3_hbm.at[pl.ds(0, first + 1)], w3.at[pl.ds(0, first + 1)], w3_sems.at[5])]

    def wave(i):
        part = pl.ds(first + 1 + i * size, size)
        return pltpu.make_async_copy(w3_hbm.at[part], w3.at[part], w3_sems.at[i])

    head = copies[0]
    head.start()
    for i in range(5):
        wave(i).start()
    used = pl.ds(ROW0, N)
    load_d = pltpu.make_async_copy(d_hbm.at[used], dx.at[used], d_sem)
    load_d.start()
    _, lam2, _ = first_means(row1[...])
    lam3, lam4, mean4 = second_means(row2[...], lam2)
    lam4_row[...] = to_row([lam4])
    head.wait()
    sweep(w3, sx, v4, spread(8.0 * lam3), spread(mean4), 3, before=lambda i: wave(i).wait())
    total5 = sweep(v4, sx, w5, spread(8.0 * lam4), None, 4, True)
    transpose_out(w5, value)
    store = pltpu.make_async_copy(value, value_hbm, value_sem)
    store.start()
    load_d.wait()
    _, odd_y = odd()
    masks = halo_masks()
    for i, at in halo_rows():
        if HALO - D_HALO <= i < HALO + D_HALO:
            fl, fr = pick(odd_y, y0[i // 4], y1[i // 4]), pick(odd_y, y1[i // 4], y0[i // 4])
            d = d_halo[i - (HALO - D_HALO)]
            dx[at, 0:K] = d[:K]
            dx[at, K:SUB] = beyond(d[K:], fl, fr, i % 4, masks, True)
    weigh(w5, dx, cs, inv, db)
    src, other = db, da
    for n in range(5):
        mass = fp(src, other, cs, 6 + n, inv if n == 4 else None)
        src, other = other, src
    sums[...] = to_row([own(total5, 4), own(mass, 10)])
    transpose_out(src, density)
    store.wait()


def finish_kernel(
    value_hbm, density_in, lam4_row, row3, value_out, density_out, ergodic_out, value_in, value, density, ergodic, sems, e_sem
):
    part = lambda i: pl.ds(4 * i, 4)
    loads = [pltpu.make_async_copy(value_hbm.at[part(i)], value_in.at[part(i)], sems.at[0, i]) for i in range(4)]
    for load in loads:
        load.start()
    shift = from_row(row3[...], 0) * (1.0 / CELLS)
    scale = CELLS / from_row(row3[...], 1)
    ergodic[...] = (lam4_row[...] + row3[...] * (2.0 / CELLS))[0, :K]
    stores = [pltpu.make_async_copy(ergodic, ergodic_out, e_sem)]
    stores[0].start()
    for i in range(4):
        for k in range(4 * i, 4 * i + 4):
            density[k] = density_in[k] * scale[k : k + 1]
        stores.append(pltpu.make_async_copy(density.at[part(i)], density_out.at[part(i)], sems.at[1, i]))
        stores[-1].start()
    for i in range(4):
        loads[i].wait()
        for k in range(4 * i, 4 * i + 4):
            value[k] = value_in[k] - shift[k : k + 1]
        stores.append(pltpu.make_async_copy(value.at[part(i)], value_out.at[part(i)], sems.at[2, i]))
        stores[-1].start()
    for store in stores:
        store.wait()


VMEM = pl.BlockSpec(memory_space=pltpu.VMEM)
HBM = pl.BlockSpec(memory_space=pltpu.HBM)
DMA = pltpu.SemaphoreType.DMA


def kernel(body, outs, ins, scratch=(), aliases=None, vmem=16):
    call = pl.pallas_call(
        body,
        out_shape=[
            pltpu.HBM(shape[0], F32) if isinstance(shape, list) else jax.ShapeDtypeStruct(shape, F32) for shape in outs
        ],
        in_specs=ins,
        out_specs=[HBM if isinstance(shape, list) else VMEM for shape in outs],
        scratch_shapes=[pltpu.VMEM(shape, F32) if isinstance(shape, tuple) else shape for shape in scratch],
        input_output_aliases=aliases or {},
        compiler_params=pltpu.CompilerParams(vmem_limit_bytes=vmem * 1024 * 1024),
    )

    def run(*operands):
        return call(*[pltpu.with_memory_space_constraint(x, pltpu.HBM) if spec is HBM else x for x, spec in zip(operands, ins)])

    return run


def exchange(first, second, axes):
    pairs = [(i, i ^ 1) for i in range(16)], [(i, (i + 1 if i % 2 else i - 1) % 16) for i in range(16)]
    return lax.ppermute(first, axes, pairs[0]), lax.ppermute(second, axes, pairs[1])


def total_over_devices(row):
    rows = jnp.broadcast_to(row[None], (DEVICES, 1, 128))
    return jnp.sum(lax.all_to_all(rows, AXES, 0, 0), axis=0)


def shards(cost, density_start, coupling):
    big = (ROWS, SUB, 128)
    row = (1, 128)
    strip = (HALO + D_HALO, K, 128)
    block = (K, N, N)
    sx, dx, x0, x1, y0, y1 = kernel(
        source_kernel,
        [big, big, strip, strip, (32, 8, 128), (32, 8, 128)],
        [HBM, HBM, HBM],
        scratch=[pltpu.SMEM((K, K), F32), block, block, DMA((2, N // CHUNK)), DMA],
    )(coupling, cost, density_start)
    y0, y1 = exchange(y0, y1, GY)
    x0, x1 = exchange(x0, x1, GX)
    sx, d_hbm, sums = kernel(
        windows_kernel, [big, [big], (3, SUB, 128)], [VMEM] * 4, scratch=[big, DMA], aliases={0: 0}
    )(sx, dx, y0, y1)
    sx, d_halo, y0, y1, sums = kernel(
        first_sums_kernel, [big, (2 * D_HALO, SUB, 128), (5, 8, 128), (5, 8, 128), row], [VMEM] * 4, aliases={0: 0}
    )(sx, sums, x0, x1)
    y0, y1 = exchange(y0, y1, GY)
    row1 = total_over_devices(sums)
    sx, w3, sums = kernel(
        second_sums_kernel, [big, [big], row], [VMEM] * 4, scratch=[big, big, DMA], aliases={0: 0}
    )(sx, y0, y1, row1)
    row2 = total_over_devices(sums)
    value, density, sums, lam4 = kernel(
        last_sums_kernel,
        [[block], block, row, row],
        [VMEM, HBM, HBM] + [VMEM] * 5,
        scratch=[big, big, big, (ROWS, 4, SUB, 128), big, big, big, big, block, DMA((6,)), DMA, DMA],
        vmem=28,
    )(sx, d_hbm, w3, d_halo, y0, y1, row1, row2)
    row3 = total_over_devices(sums)
    value, density, ergodic = kernel(
        finish_kernel,
        [[block], [block], [(K,)]],
        [HBM] + [VMEM] * 3,
        scratch=[block, block, block, (K,), DMA((3, 4)), DMA],
    )(value, density, lam4, row3)
    return value, density, ergodic


def solution(mesh):
    torus = Mesh(mesh.devices.reshape(4, 2, 2, 2, 8), AXES)
    specs = (P(None, GX, GY), P(None, GX, GY), P())
    return jax.shard_map(shards, mesh=torus, in_specs=specs, out_specs=specs, check_vma=False)
```

```python
import functools

import jax
import jax.numpy as jnp
from jax import lax
from jax.experimental import pallas as pl
from jax.experimental.pallas import tpu as pltpu
from jax.sharding import Mesh
from jax.sharding import PartitionSpec as P

HALO = 10
D_HALO = 5
PAD = 4
ROW0 = PAD + HALO
N = 128
ROWS = N + 2 * ROW0
K = 16
SUB = 24
AXES = ("y", "xh", "c", "xl", "z")
GX = ("y", "xh", "c")
GY = ("xl", "z")
DEVICES = 256
CELLS = 2048.0 * 2048.0
SLOT = (0, 16, 64, 80)
BLOCK = 50
WEIGH = 32
FP = 72
SUMS = 64
GROUPS = 16
CHUNK = 32
WAVE = 29
F32 = jnp.float32


def lanes(shape):
    return lax.broadcasted_iota(jnp.int32, shape, 1)


def roll(x, shift):
    return pltpu.roll(x, shift % 128, 1)


def between(lane, low, high):
    return (lane >= low) & (lane < high)


def recip(x):
    return 1.0 / x


def odd():
    return lax.axis_index("c") == 1, lax.axis_index("z") % 2 == 1


def pick(flag, yes, no):
    return jnp.where(jnp.broadcast_to(flag, yes.shape), yes, no)


def pack(rows, left):
    lane = lanes((8, 128))
    out = jnp.zeros((8, 128), F32)
    for (s0, s1, d0, d1), base in zip(rows, SLOT):
        for half, (s, d) in enumerate(((s0, d0), (s1, d1))):
            at = base + 32 * half
            ds = roll(s, at if left else at + HALO)
            dd = roll(d, at + HALO if left else at + HALO + D_HALO)
            out = jnp.where(between(lane, at, at + HALO), ds, out)
            out = jnp.where(between(lane, at + HALO, at + HALO + D_HALO), dd, out)
    return out


def windows(a, b):
    lane = lanes((8, 128))
    left = jnp.where(lane < 32, roll(a, 10), roll(b, 42))
    right = jnp.where(lane < 96, roll(a, 86), roll(b, 118))
    return jnp.where(lane < 64, left, right)


def halo_masks():
    lane = lanes((8, 128))
    left = between(lane, 0, 10) | between(lane, 32, 42)
    right = between(lane, 86, 96) | between(lane, 118, 128)
    return left, right


def beyond(window, from_left, from_right, i, masks, density):
    base = SLOT[i]
    a = roll(from_left, -base - 5 if density else -base)
    b = roll(from_right, 76 - base if density else 86 - base)
    return jnp.where(masks[0], a, jnp.where(masks[1], b, window))


def own(total, margin):
    lane = lanes((K, 128))
    main = jnp.where(between(lane, margin, N - margin), total[:K], 0.0)
    main = jnp.sum(main, axis=1, keepdims=True)
    if margin == 0:
        return main
    edge = total[K:]
    lane = lanes((8, 128))
    halves = []
    for half in range(2):
        at = 32 * half
        mask = between(lane, at + 10, at + 10 + margin) | between(lane, 64 + at + 22 - margin, 64 + at + 22)
        halves.append(jnp.sum(jnp.where(mask, edge, 0.0), axis=1, keepdims=True))
    return main + jnp.concatenate(halves, axis=0)


def to_row(columns):
    lane, cls = lanes((K, 128)), lax.broadcasted_iota(jnp.int32, (K, 128), 0)
    grid = jnp.zeros((K, 128), F32)
    for i, column in enumerate(columns):
        grid = jnp.where(lane == cls + K * i, column, grid)
    return jnp.sum(grid, axis=0, keepdims=True)


def from_row(row, i):
    lane, cls = lanes((K, 128)), lax.broadcasted_iota(jnp.int32, (K, 128), 0)
    return jnp.sum(jnp.where(lane == cls + K * i, row, 0.0), axis=1, keepdims=True)


def spread(column):
    wide = jnp.broadcast_to(column, (K, 128))
    lane = lanes((8, 128))
    edge = jnp.where((lane // 32) % 2 == 0, wide[:8], wide[8:])
    return jnp.concatenate([wide, edge], axis=0)


def parts(up, mid, down, s):
    left, right = roll(mid, 1), roll(mid, -1)
    px = 2.0 + jnp.abs(up - down)
    py = 2.0 + jnp.abs(left - right)
    n = s + (px * (2.0 * (up + down) + (4.0 - px)) + py * (2.0 * (left + right) + (4.0 - py)))
    return n, recip(px + py)


def row_loop(first, count, body, init=0, before=None, block=None):
    blocks = -(-count // (block or BLOCK))
    size = -(-count // blocks)
    first = first - (blocks * size - count) // 2

    def step(i, carry):
        if before is not None:
            before(i)
        return body(first + i * size, size, carry)

    return lax.fori_loop(0, blocks, step, init)


def sweep(src, s_ref, dst, lam8, minus, margin, summed=False, before=None, half=False):
    def body(r, size, total):
        rows = [src[r - 1 + i] for i in range(size + 2)]
        if half:
            rows = [row * 0.0625 + 0.5 for row in rows]
        for i in range(size):
            n, inv = parts(rows[i], rows[i + 1], rows[i + 2], s_ref[r + i] - lam8)
            w = n * (0.25 * inv)
            if minus is not None:
                w = w - minus
            dst[r + i] = w
        return total

    row_loop(PAD + margin, ROWS - 2 * (PAD + margin), body, before=before, block=32 if before else None)
    if summed:
        def add(r, size, total):
            for i in range(size):
                total = total + dst[r + i]
            return total

        return row_loop(ROW0, N, add, jnp.zeros((SUB, 128), F32), block=SUMS)


def sweep_sums(src, s_ref, half, first=ROW0, count=N):
    def body(r, size, carry):
        a, b = carry
        rows = [src[r - 1 + i] for i in range(size + 2)]
        if half:
            rows = [row * 0.0625 + 0.5 for row in rows]
        for i in range(size):
            n, inv = parts(rows[i], rows[i + 1], rows[i + 2], s_ref[r + i])
            a = a + n * inv
            b = b + inv
        return a, b

    zero = jnp.zeros((SUB, 128), F32)
    return row_loop(first, count, body, (zero, zero), block=count // 2)


def source_kernel(c_hbm, cost_hbm, d_hbm, sx, dx, x0, x1, y0, y1, c_ref, cost_ref, d_ref, sems, c_sem):
    odd_x, odd_y = odd()
    s2, d2 = sx.reshape(ROWS * SUB, 128), dx.reshape(ROWS * SUB, 128)
    coupling = pltpu.make_async_copy(c_hbm, c_ref, c_sem)
    coupling.start()

    def copies(i):
        part = pl.ds(pl.multiple_of(i * CHUNK, CHUNK), CHUNK)
        return (
            pltpu.make_async_copy(d_hbm.at[:, part], d_ref.at[:, part], sems.at[0, i]),
            pltpu.make_async_copy(cost_hbm.at[:, part], cost_ref.at[:, part], sems.at[1, i]),
        )

    for i in range(N // CHUNK):
        for copy in copies(i):
            copy.start()
    coupling.wait()

    def chunk(i, carry):
        for copy in copies(i):
            copy.wait()
        for part in range(CHUNK // 8):
            r = pl.multiple_of(i * CHUNK + part * 8, 8)
            dens = [d_ref[j, pl.ds(r, 8), :] for j in range(K)]
            base = (ROW0 + r) * SUB
            for j in range(K):
                d2[pl.ds(base + j, 8, stride=SUB), :] = dens[j]
            for k in range(K):
                acc = cost_ref[k, pl.ds(r, 8), :]
                for j in range(K):
                    acc = acc + c_ref[k, j] * dens[j]
                s2[pl.ds(base + k, 8, stride=SUB), :] = acc * 8.0 - 8.0
        for g in range(CHUNK // 4):
            g = i * (CHUNK // 4) + g
            r = ROW0 + g * 4
            rows = [(sx[r + i, 0:8], sx[r + i, 8:16], dx[r + i, 0:8], dx[r + i, 8:16]) for i in range(4)]
            left, right = pack(rows, True), pack(rows, False)
            y0[g] = pick(odd_y, left, right)
            y1[g] = pick(odd_y, right, left)
        return carry

    lax.fori_loop(0, N // CHUNK, chunk, 0)

    tops = [sx[ROW0 + i, 0:K] for i in range(HALO)] + [dx[ROW0 + i, 0:K] for i in range(D_HALO)]
    last = ROW0 + N
    bottoms = [sx[last - HALO + i, 0:K] for i in range(HALO)] + [dx[last - D_HALO + i, 0:K] for i in range(D_HALO)]
    for i, (top, bottom) in enumerate(zip(tops, bottoms)):
        x0[i] = pick(odd_x, top, bottom)
        x1[i] = pick(odd_x, bottom, top)


def halo_rows():
    return [(i, PAD + i) for i in range(HALO)] + [(HALO + i, ROW0 + N + i) for i in range(HALO)]


def windows_kernel(s_in, d_in, y0, y1, sx, d_hbm, sums, dx, d_sem):
    del s_in
    _, odd_y = odd()
    masks = halo_masks()

    def d_group(g0, carry):
        for g in range(GROUPS):
            g = g0 * GROUPS + g
            fl, fr = pick(odd_y, y0[g], y1[g]), pick(odd_y, y1[g], y0[g])
            for i in range(4):
                r = ROW0 + g * 4 + i
                d = d_in[r, 0:K]
                dx[r, 0:K] = d
                dx[r, K:SUB] = beyond(windows(d[:8], d[8:]), fl, fr, i, masks, True)
        return carry

    lax.fori_loop(0, N // 4 // GROUPS, d_group, 0)
    used = pl.ds(ROW0, N)
    store_d = pltpu.make_async_copy(dx.at[used], d_hbm.at[used], d_sem)
    store_d.start()

    def group(g0, total):
        for g in range(GROUPS):
            g = g0 * GROUPS + g
            fl, fr = pick(odd_y, y0[g], y1[g]), pick(odd_y, y1[g], y0[g])
            for i in range(4):
                r = ROW0 + g * 4 + i
                s = sx[r, 0:K]
                total = total + s
                sx[r, K:SUB] = beyond(windows(s[:8], s[8:]), fl, fr, i, masks, False)
        return total

    total = lax.fori_loop(0, N // 4 // GROUPS, group, jnp.zeros((K, 128), F32))
    a, b = sweep_sums(sx, sx, True, ROW0 + 1, N - 2)
    sums[0, 0:K] = total
    sums[1] = a
    sums[2] = b
    store_d.wait()


def first_sums_kernel(s_in, sums_in, x0, x1, sx, d_halo, y0, y1, sums):
    del s_in
    odd_x, odd_y = odd()
    zero = jnp.zeros((8, 128), F32)
    packed = []
    for i, at in halo_rows():
        above, below = (x0, x1), (x1, x0)
        yes, no = above if i < HALO else below
        s = pick(odd_x, yes[i % HALO], no[i % HALO])
        sx[at, 0:K] = s
        sx[at, K:SUB] = windows(s[:8], s[8:])
        if HALO - D_HALO <= i < HALO + D_HALO:
            j = HALO + i % D_HALO
            d = pick(odd_x, yes[j], no[j])
            d_halo[i - (HALO - D_HALO), 0:K] = d
            d_halo[i - (HALO - D_HALO), K:SUB] = windows(d[:8], d[8:])
            packed.append((s[:8], s[8:], d[:8], d[8:]))
        else:
            packed.append((s[:8], s[8:], zero, zero))
    for g in range(5):
        rows = packed[4 * g : 4 * g + 4]
        left, right = pack(rows, True), pack(rows, False)
        y0[g] = pick(odd_y, left, right)
        y1[g] = pick(odd_y, right, left)
    a, b = sums_in[1], sums_in[2]
    for r in (ROW0, ROW0 + N - 1):
        up, mid, down = [sx[r + i] * 0.0625 + 0.5 for i in (-1, 0, 1)]
        n, inv = parts(up, mid, down, sx[r])
        a = a + n * inv
        b = b + inv
    sums[...] = to_row([jnp.sum(sums_in[0, 0:K], axis=1, keepdims=True), own(a, 1), own(b, 1)])


def first_means(row):
    lam1 = from_row(row, 0) * (0.125 / CELLS) + 1.0
    mean2 = from_row(row, 1) * (0.25 / CELLS) - lam1 * (from_row(row, 2) * (2.0 / CELLS))
    return lam1, 2.0 * mean2, mean2


def second_means(row, lam2):
    lam3 = lam2 + from_row(row, 0) * (2.0 / CELLS)
    mean4 = from_row(row, 1) * (0.25 / CELLS) - lam3 * (from_row(row, 2) * (2.0 / CELLS))
    return lam3, lam2 + 2.0 * mean4, mean4


def second_sums_kernel(s_in, y0, y1, row1, sx, w3_hbm, sums, v2, w3, sem):
    del s_in
    _, odd_y = odd()
    masks = halo_masks()
    for i, at in halo_rows():
        fl, fr = pick(odd_y, y0[i // 4], y1[i // 4]), pick(odd_y, y1[i // 4], y0[i // 4])
        sx[at, K:SUB] = beyond(sx[at, K:SUB], fl, fr, i % 4, masks, False)

    lam1, lam2, mean2 = first_means(row1[...])
    sweep(sx, sx, v2, spread(8.0 * lam1), spread(mean2), 1, half=True)
    total = sweep(v2, sx, w3, spread(8.0 * lam2), None, 2, True)
    store = pltpu.make_async_copy(w3, w3_hbm, sem)
    store.start()
    a, b = sweep_sums(w3, sx, False)
    sums[...] = to_row([own(total, 2), own(a, 3), own(b, 3)])
    store.wait()


def transpose_out(src, scratch, out):
    lane = lanes((8, 128))
    low, high = lane < 10, lane >= 118
    flat = scratch.reshape(2 * 32 * K, 128)

    def body(g, carry):
        slot = 32 * (g % 2)
        for i in range(32):
            r = g * 32 + i
            e = src[ROW0 + r, K:SUB]
            for half in range(2):
                a = src[ROW0 + r, 8 * half : 8 * half + 8]
                left = roll(e, -10 - 32 * half)
                right = roll(e, 42 - 32 * half)
                scratch[slot + i, 8 * half : 8 * half + 8] = jnp.where(low, left, jnp.where(high, right, a))
            if i % 8 == 7:
                at = pl.multiple_of(g * 32 + i - 7, 8)
                for k in range(K):
                    out[k, pl.ds(at, 8), :] = flat[pl.ds((slot + i - 7) * K + k, 8, stride=K), :]
        return carry

    lax.fori_loop(0, N // 32, body, 0)


def weigh(w5, d, cs, inv_ref, s0):
    def body(r, size, carry):
        rows = [w5[r - 1 + i] for i in range(size + 2)]
        for i in range(size):
            u = rows[i + 1]
            dx, dy = rows[i] - rows[i + 2], roll(u, 1) - roll(u, -1)
            xp, yp = jnp.maximum(dx, 0.0), jnp.maximum(dy, 0.0)
            xm, ym = xp - dx, yp - dy
            t = 4.0 + ((xp + xm) + (yp + ym))
            inv = recip(t)
            inv_ref[r + i] = inv
            s0[r + i] = d[r + i] * t
            for n, p in enumerate((xp, xm, yp, ym)):
                cs[r + i, n] = inv + p * inv
        return carry

    row_loop(PAD + 5, ROWS - 2 * (PAD + 5), body, block=WEIGH)


def fp(src, dst, cs, margin, inv_ref=None):
    def body(r, size, total):
        rows = [src[r - 1 + i] for i in range(size + 2)]
        for i in range(size):
            u = rows[i + 1]
            along_x = cs[r + i - 1, 0] * rows[i] + cs[r + i + 1, 1] * rows[i + 2]
            along_y = roll(cs[r + i, 2] * u, 1) + roll(cs[r + i, 3] * u, -1)
            fresh = along_x + along_y
            if inv_ref is not None:
                fresh = fresh * inv_ref[r + i]
                total = total + fresh
            dst[r + i] = fresh
        return total

    return row_loop(PAD + margin, ROWS - 2 * (PAD + margin), body, jnp.zeros((SUB, 128), F32), block=FP)


def last_sums_kernel(
    sx, d_hbm, w3_hbm, d_halo, y0, y1, row1, row2, value_hbm, density, sums, lam4_row,
    w3, v4, w5, cs, dx, da, db, inv, scratch, value, w3_sems, d_sem, value_sem,
):
    size = WAVE
    first = PAD + 2
    copies = [pltpu.make_async_copy(w3_hbm.at[pl.ds(0, first + 1)], w3.at[pl.ds(0, first + 1)], w3_sems.at[5])]

    def wave(i):
        part = pl.ds(first + 1 + i * size, size)
        return pltpu.make_async_copy(w3_hbm.at[part], w3.at[part], w3_sems.at[i])

    head = copies[0]
    head.start()
    for i in range(5):
        wave(i).start()
    used = pl.ds(ROW0, N)
    load_d = pltpu.make_async_copy(d_hbm.at[used], dx.at[used], d_sem)
    load_d.start()
    _, lam2, _ = first_means(row1[...])
    lam3, lam4, mean4 = second_means(row2[...], lam2)
    lam4_row[...] = to_row([lam4])
    head.wait()
    sweep(w3, sx, v4, spread(8.0 * lam3), spread(mean4), 3, before=lambda i: wave(i).wait())
    total5 = sweep(v4, sx, w5, spread(8.0 * lam4), None, 4, True)
    transpose_out(w5, scratch, value)
    store = pltpu.make_async_copy(value, value_hbm, value_sem)
    store.start()
    load_d.wait()
    _, odd_y = odd()
    masks = halo_masks()
    for i, at in halo_rows():
        if HALO - D_HALO <= i < HALO + D_HALO:
            fl, fr = pick(odd_y, y0[i // 4], y1[i // 4]), pick(odd_y, y1[i // 4], y0[i // 4])
            d = d_halo[i - (HALO - D_HALO)]
            dx[at, 0:K] = d[:K]
            dx[at, K:SUB] = beyond(d[K:], fl, fr, i % 4, masks, True)
    weigh(w5, dx, cs, inv, db)
    src, other = db, da
    for n in range(5):
        mass = fp(src, other, cs, 6 + n, inv if n == 4 else None)
        src, other = other, src
    sums[...] = to_row([own(total5, 4), own(mass, 10)])
    transpose_out(src, scratch, density)
    store.wait()


def finish_kernel(
    value_hbm, density_in, lam4_row, row3, value_out, density_out, ergodic_out, value_in, value, density, ergodic, sems, e_sem
):
    part = lambda i: pl.ds(4 * i, 4)
    loads = [pltpu.make_async_copy(value_hbm.at[part(i)], value_in.at[part(i)], sems.at[0, i]) for i in range(4)]
    for load in loads:
        load.start()
    shift = from_row(row3[...], 0) * (1.0 / CELLS)
    scale = CELLS / from_row(row3[...], 1)
    ergodic[...] = (lam4_row[...] + row3[...] * (2.0 / CELLS))[0, :K]
    stores = [pltpu.make_async_copy(ergodic, ergodic_out, e_sem)]
    stores[0].start()
    for i in range(4):
        for k in range(4 * i, 4 * i + 4):
            density[k] = density_in[k] * scale[k : k + 1]
        stores.append(pltpu.make_async_copy(density.at[part(i)], density_out.at[part(i)], sems.at[1, i]))
        stores[-1].start()
    for i in range(4):
        loads[i].wait()
        for k in range(4 * i, 4 * i + 4):
            value[k] = value_in[k] - shift[k : k + 1]
        stores.append(pltpu.make_async_copy(value.at[part(i)], value_out.at[part(i)], sems.at[2, i]))
        stores[-1].start()
    for store in stores:
        store.wait()


VMEM = pl.BlockSpec(memory_space=pltpu.VMEM)
HBM = pl.BlockSpec(memory_space=pltpu.HBM)
DMA = pltpu.SemaphoreType.DMA


def kernel(body, outs, ins, scratch=(), aliases=None, vmem=16):
    call = pl.pallas_call(
        body,
        out_shape=[
            pltpu.HBM(shape[0], F32) if isinstance(shape, list) else jax.ShapeDtypeStruct(shape, F32) for shape in outs
        ],
        in_specs=ins,
        out_specs=[HBM if isinstance(shape, list) else VMEM for shape in outs],
        scratch_shapes=[pltpu.VMEM(shape, F32) if isinstance(shape, tuple) else shape for shape in scratch],
        input_output_aliases=aliases or {},
        compiler_params=pltpu.CompilerParams(vmem_limit_bytes=vmem * 1024 * 1024),
    )

    def run(*operands):
        return call(*[pltpu.with_memory_space_constraint(x, pltpu.HBM) if spec is HBM else x for x, spec in zip(operands, ins)])

    return run


def exchange(first, second, axes):
    pairs = [(i, i ^ 1) for i in range(16)], [(i, (i + 1 if i % 2 else i - 1) % 16) for i in range(16)]
    return lax.ppermute(first, axes, pairs[0]), lax.ppermute(second, axes, pairs[1])


def total_over_devices(row):
    rows = jnp.broadcast_to(row[None], (DEVICES, 1, 128))
    return jnp.sum(lax.all_to_all(rows, AXES, 0, 0), axis=0)


def shards(cost, density_start, coupling):
    big = (ROWS, SUB, 128)
    row = (1, 128)
    strip = (HALO + D_HALO, K, 128)
    block = (K, N, N)
    sx, dx, x0, x1, y0, y1 = kernel(
        source_kernel,
        [big, big, strip, strip, (32, 8, 128), (32, 8, 128)],
        [HBM, HBM, HBM],
        scratch=[pltpu.SMEM((K, K), F32), block, block, DMA((2, N // CHUNK)), DMA],
    )(coupling, cost, density_start)
    y0, y1 = exchange(y0, y1, GY)
    x0, x1 = exchange(x0, x1, GX)
    sx, d_hbm, sums = kernel(
        windows_kernel, [big, [big], (3, SUB, 128)], [VMEM] * 4, scratch=[big, DMA], aliases={0: 0}
    )(sx, dx, y0, y1)
    sx, d_halo, y0, y1, sums = kernel(
        first_sums_kernel, [big, (2 * D_HALO, SUB, 128), (5, 8, 128), (5, 8, 128), row], [VMEM] * 4, aliases={0: 0}
    )(sx, sums, x0, x1)
    y0, y1 = exchange(y0, y1, GY)
    sums, y0, y1 = lax.optimization_barrier((sums, y0, y1))
    row1 = total_over_devices(sums)
    sx, w3, sums = kernel(
        second_sums_kernel, [big, [big], row], [VMEM] * 4, scratch=[big, big, DMA], aliases={0: 0}
    )(sx, y0, y1, row1)
    row2 = total_over_devices(sums)
    value, density, sums, lam4 = kernel(
        last_sums_kernel,
        [[block], block, row, row],
        [VMEM, HBM, HBM] + [VMEM] * 5,
        scratch=[big, big, big, (ROWS, 4, SUB, 128), big, big, big, big, (64, K, 128), block, DMA((6,)), DMA, DMA],
        vmem=28,
    )(sx, d_hbm, w3, d_halo, y0, y1, row1, row2)
    row3 = total_over_devices(sums)
    value, density, ergodic = kernel(
        finish_kernel,
        [[block], [block], [(K,)]],
        [HBM] + [VMEM] * 3,
        scratch=[block, block, block, (K,), DMA((3, 4)), DMA],
    )(value, density, lam4, row3)
    return value, density, ergodic


def solution(mesh):
    torus = Mesh(mesh.devices.reshape(4, 2, 2, 2, 8), AXES)
    specs = (P(None, GX, GY), P(None, GX, GY), P())
    return jax.shard_map(shards, mesh=torus, in_specs=specs, out_specs=specs, check_vma=False)
```

```python
import functools

import jax
import jax.numpy as jnp
from jax import lax
from jax.experimental import pallas as pl
from jax.experimental.pallas import tpu as pltpu
from jax.sharding import Mesh
from jax.sharding import PartitionSpec as P

HALO = 10
D_HALO = 5
PAD = 4
ROW0 = PAD + HALO
N = 128
ROWS = N + 2 * ROW0
K = 16
SUB = 24
AXES = ("y", "xh", "c", "xl", "z")
GX = ("y", "xh", "c")
GY = ("xl", "z")
DEVICES = 256
CELLS = 2048.0 * 2048.0
SLOT = (0, 16, 64, 80)
BLOCK = 50
WEIGH = 32
FP = 72
SUMS = 64
GROUPS = 16
CHUNK = 32
WAVE = 29
F32 = jnp.float32


def lanes(shape):
    return lax.broadcasted_iota(jnp.int32, shape, 1)


def roll(x, shift):
    return pltpu.roll(x, shift % 128, 1)


def between(lane, low, high):
    return (lane >= low) & (lane < high)


def recip(x):
    return 1.0 / x


def odd():
    return lax.axis_index("c") == 1, lax.axis_index("z") % 2 == 1


def pick(flag, yes, no):
    return jnp.where(jnp.broadcast_to(flag, yes.shape), yes, no)


def pack(rows, left):
    lane = lanes((8, 128))
    out = jnp.zeros((8, 128), F32)
    for (s0, s1, d0, d1), base in zip(rows, SLOT):
        for half, (s, d) in enumerate(((s0, d0), (s1, d1))):
            at = base + 32 * half
            ds = roll(s, at if left else at + HALO)
            dd = roll(d, at + HALO if left else at + HALO + D_HALO)
            out = jnp.where(between(lane, at, at + HALO), ds, out)
            out = jnp.where(between(lane, at + HALO, at + HALO + D_HALO), dd, out)
    return out


def windows(a, b):
    lane = lanes((8, 128))
    left = jnp.where(lane < 32, roll(a, 10), roll(b, 42))
    right = jnp.where(lane < 96, roll(a, 86), roll(b, 118))
    return jnp.where(lane < 64, left, right)


def halo_masks():
    lane = lanes((8, 128))
    left = between(lane, 0, 10) | between(lane, 32, 42)
    right = between(lane, 86, 96) | between(lane, 118, 128)
    return left, right


def beyond(window, from_left, from_right, i, masks, density):
    base = SLOT[i]
    a = roll(from_left, -base - 5 if density else -base)
    b = roll(from_right, 76 - base if density else 86 - base)
    return jnp.where(masks[0], a, jnp.where(masks[1], b, window))


def own(total, margin):
    lane = lanes((K, 128))
    main = jnp.where(between(lane, margin, N - margin), total[:K], 0.0)
    main = jnp.sum(main, axis=1, keepdims=True)
    if margin == 0:
        return main
    edge = total[K:]
    lane = lanes((8, 128))
    halves = []
    for half in range(2):
        at = 32 * half
        mask = between(lane, at + 10, at + 10 + margin) | between(lane, 64 + at + 22 - margin, 64 + at + 22)
        halves.append(jnp.sum(jnp.where(mask, edge, 0.0), axis=1, keepdims=True))
    return main + jnp.concatenate(halves, axis=0)


def to_row(columns):
    lane, cls = lanes((K, 128)), lax.broadcasted_iota(jnp.int32, (K, 128), 0)
    grid = jnp.zeros((K, 128), F32)
    for i, column in enumerate(columns):
        grid = jnp.where(lane == cls + K * i, column, grid)
    return jnp.sum(grid, axis=0, keepdims=True)


def from_row(row, i):
    lane, cls = lanes((K, 128)), lax.broadcasted_iota(jnp.int32, (K, 128), 0)
    return jnp.sum(jnp.where(lane == cls + K * i, row, 0.0), axis=1, keepdims=True)


def spread(column):
    wide = jnp.broadcast_to(column, (K, 128))
    lane = lanes((8, 128))
    edge = jnp.where((lane // 32) % 2 == 0, wide[:8], wide[8:])
    return jnp.concatenate([wide, edge], axis=0)


def parts(up, mid, down, s):
    left, right = roll(mid, 1), roll(mid, -1)
    px = 2.0 + jnp.abs(up - down)
    py = 2.0 + jnp.abs(left - right)
    n = s + (px * (2.0 * (up + down) + (4.0 - px)) + py * (2.0 * (left + right) + (4.0 - py)))
    return n, recip(px + py)


def row_loop(first, count, body, init=0, before=None, block=None):
    blocks = -(-count // (block or BLOCK))
    size = -(-count // blocks)
    first = first - (blocks * size - count) // 2

    def step(i, carry):
        if before is not None:
            before(i)
        return body(first + i * size, size, carry)

    return lax.fori_loop(0, blocks, step, init)


def sweep(src, s_ref, dst, lam8, minus, margin, summed=False, before=None, half=False):
    def body(r, size, total):
        rows = [src[r - 1 + i] for i in range(size + 2)]
        if half:
            rows = [row * 0.0625 + 0.5 for row in rows]
        for i in range(size):
            n, inv = parts(rows[i], rows[i + 1], rows[i + 2], s_ref[r + i] - lam8)
            w = n * (0.25 * inv)
            if minus is not None:
                w = w - minus
            dst[r + i] = w
        return total

    row_loop(PAD + margin, ROWS - 2 * (PAD + margin), body, before=before, block=32 if before else None)
    if summed:
        def add(r, size, total):
            for i in range(size):
                total = total + dst[r + i]
            return total

        return row_loop(ROW0, N, add, jnp.zeros((SUB, 128), F32), block=SUMS)


def sweep_sums(src, s_ref, half, first=ROW0, count=N):
    def body(r, size, carry):
        a, b = carry
        rows = [src[r - 1 + i] for i in range(size + 2)]
        if half:
            rows = [row * 0.0625 + 0.5 for row in rows]
        for i in range(size):
            n, inv = parts(rows[i], rows[i + 1], rows[i + 2], s_ref[r + i])
            a = a + n * inv
            b = b + inv
        return a, b

    zero = jnp.zeros((SUB, 128), F32)
    return row_loop(first, count, body, (zero, zero), block=count // 2)


def source_kernel(c_hbm, cost_hbm, d_hbm, sx, dx, x0, x1, y0, y1, c_ref, cost_ref, d_ref, sems, c_sem):
    odd_x, odd_y = odd()
    s2, d2 = sx.reshape(ROWS * SUB, 128), dx.reshape(ROWS * SUB, 128)
    coupling = pltpu.make_async_copy(c_hbm, c_ref, c_sem)
    coupling.start()

    def copies(i):
        part = pl.ds(pl.multiple_of(i * CHUNK, CHUNK), CHUNK)
        return (
            pltpu.make_async_copy(d_hbm.at[:, part], d_ref.at[:, part], sems.at[0, i]),
            pltpu.make_async_copy(cost_hbm.at[:, part], cost_ref.at[:, part], sems.at[1, i]),
        )

    for i in range(N // CHUNK):
        for copy in copies(i):
            copy.start()
    coupling.wait()

    def chunk(i, carry):
        for copy in copies(i):
            copy.wait()
        for part in range(CHUNK // 8):
            r = pl.multiple_of(i * CHUNK + part * 8, 8)
            dens = [d_ref[j, pl.ds(r, 8), :] for j in range(K)]
            base = (ROW0 + r) * SUB
            for j in range(K):
                d2[pl.ds(base + j, 8, stride=SUB), :] = dens[j]
            for k in range(K):
                acc = cost_ref[k, pl.ds(r, 8), :]
                for j in range(K):
                    acc = acc + c_ref[k, j] * dens[j]
                s2[pl.ds(base + k, 8, stride=SUB), :] = acc * 8.0 - 8.0
        for g in range(CHUNK // 4):
            g = i * (CHUNK // 4) + g
            r = ROW0 + g * 4
            rows = [(sx[r + i, 0:8], sx[r + i, 8:16], dx[r + i, 0:8], dx[r + i, 8:16]) for i in range(4)]
            left, right = pack(rows, True), pack(rows, False)
            y0[g] = pick(odd_y, left, right)
            y1[g] = pick(odd_y, right, left)
        return carry

    lax.fori_loop(0, N // CHUNK, chunk, 0)

    tops = [sx[ROW0 + i, 0:K] for i in range(HALO)] + [dx[ROW0 + i, 0:K] for i in range(D_HALO)]
    last = ROW0 + N
    bottoms = [sx[last - HALO + i, 0:K] for i in range(HALO)] + [dx[last - D_HALO + i, 0:K] for i in range(D_HALO)]
    for i, (top, bottom) in enumerate(zip(tops, bottoms)):
        x0[i] = pick(odd_x, top, bottom)
        x1[i] = pick(odd_x, bottom, top)


def halo_rows():
    return [(i, PAD + i) for i in range(HALO)] + [(HALO + i, ROW0 + N + i) for i in range(HALO)]


def windows_kernel(s_in, d_in, y0, y1, sx, d_hbm, sums, dx, d_sem):
    del s_in
    _, odd_y = odd()
    masks = halo_masks()

    def d_group(g0, carry):
        for g in range(GROUPS):
            g = g0 * GROUPS + g
            fl, fr = pick(odd_y, y0[g], y1[g]), pick(odd_y, y1[g], y0[g])
            for i in range(4):
                r = ROW0 + g * 4 + i
                d = d_in[r, 0:K]
                dx[r, 0:K] = d
                dx[r, K:SUB] = beyond(windows(d[:8], d[8:]), fl, fr, i, masks, True)
        return carry

    lax.fori_loop(0, N // 4 // GROUPS, d_group, 0)
    used = pl.ds(ROW0, N)
    store_d = pltpu.make_async_copy(dx.at[used], d_hbm.at[used], d_sem)
    store_d.start()

    def group(g0, total):
        for g in range(GROUPS):
            g = g0 * GROUPS + g
            fl, fr = pick(odd_y, y0[g], y1[g]), pick(odd_y, y1[g], y0[g])
            for i in range(4):
                r = ROW0 + g * 4 + i
                s = sx[r, 0:K]
                total = total + s
                sx[r, K:SUB] = beyond(windows(s[:8], s[8:]), fl, fr, i, masks, False)
        return total

    total = lax.fori_loop(0, N // 4 // GROUPS, group, jnp.zeros((K, 128), F32))
    a, b = sweep_sums(sx, sx, True, ROW0 + 1, N - 2)
    sums[0, 0:K] = total
    sums[1] = a
    sums[2] = b
    store_d.wait()


def first_sums_kernel(s_in, sums_in, x0, x1, sx, d_halo, y0, y1, sums):
    del s_in
    odd_x, odd_y = odd()
    zero = jnp.zeros((8, 128), F32)
    packed = []
    for i, at in halo_rows():
        above, below = (x0, x1), (x1, x0)
        yes, no = above if i < HALO else below
        s = pick(odd_x, yes[i % HALO], no[i % HALO])
        sx[at, 0:K] = s
        sx[at, K:SUB] = windows(s[:8], s[8:])
        if HALO - D_HALO <= i < HALO + D_HALO:
            j = HALO + i % D_HALO
            d = pick(odd_x, yes[j], no[j])
            d_halo[i - (HALO - D_HALO), 0:K] = d
            d_halo[i - (HALO - D_HALO), K:SUB] = windows(d[:8], d[8:])
            packed.append((s[:8], s[8:], d[:8], d[8:]))
        else:
            packed.append((s[:8], s[8:], zero, zero))
    for g in range(5):
        rows = packed[4 * g : 4 * g + 4]
        left, right = pack(rows, True), pack(rows, False)
        y0[g] = pick(odd_y, left, right)
        y1[g] = pick(odd_y, right, left)
    a, b = sums_in[1], sums_in[2]
    for r in (ROW0, ROW0 + N - 1):
        up, mid, down = [sx[r + i] * 0.0625 + 0.5 for i in (-1, 0, 1)]
        n, inv = parts(up, mid, down, sx[r])
        a = a + n * inv
        b = b + inv
    sums[...] = to_row([jnp.sum(sums_in[0, 0:K], axis=1, keepdims=True), own(a, 1), own(b, 1)])


def first_means(row):
    lam1 = from_row(row, 0) * (0.125 / CELLS) + 1.0
    mean2 = from_row(row, 1) * (0.25 / CELLS) - lam1 * (from_row(row, 2) * (2.0 / CELLS))
    return lam1, 2.0 * mean2, mean2


def second_means(row, lam2):
    lam3 = lam2 + from_row(row, 0) * (2.0 / CELLS)
    mean4 = from_row(row, 1) * (0.25 / CELLS) - lam3 * (from_row(row, 2) * (2.0 / CELLS))
    return lam3, lam2 + 2.0 * mean4, mean4


def second_sums_kernel(s_in, y0, y1, row1, sx, w3_hbm, sums, v2, w3, sem):
    del s_in
    _, odd_y = odd()
    masks = halo_masks()
    for i, at in halo_rows():
        fl, fr = pick(odd_y, y0[i // 4], y1[i // 4]), pick(odd_y, y1[i // 4], y0[i // 4])
        sx[at, K:SUB] = beyond(sx[at, K:SUB], fl, fr, i % 4, masks, False)

    lam1, lam2, mean2 = first_means(row1[...])
    sweep(sx, sx, v2, spread(8.0 * lam1), spread(mean2), 1, half=True)
    total = sweep(v2, sx, w3, spread(8.0 * lam2), None, 2, True)
    store = pltpu.make_async_copy(w3, w3_hbm, sem)
    store.start()
    a, b = sweep_sums(w3, sx, False)
    sums[...] = to_row([own(total, 2), own(a, 3), own(b, 3)])
    store.wait()


def transpose_out(src, scratch, out):
    lane = lanes((8, 128))
    low, high = lane < 10, lane >= 118
    flat = scratch.reshape(2 * 32 * K, 128)

    def body(g, carry):
        slot = 32 * (g % 2)
        for i in range(32):
            r = g * 32 + i
            e = src[ROW0 + r, K:SUB]
            for half in range(2):
                a = src[ROW0 + r, 8 * half : 8 * half + 8]
                left = roll(e, -10 - 32 * half)
                right = roll(e, 42 - 32 * half)
                scratch[slot + i, 8 * half : 8 * half + 8] = jnp.where(low, left, jnp.where(high, right, a))
            if i % 8 == 7:
                at = pl.multiple_of(g * 32 + i - 7, 8)
                for k in range(K):
                    out[k, pl.ds(at, 8), :] = flat[pl.ds((slot + i - 7) * K + k, 8, stride=K), :]
        return carry

    lax.fori_loop(0, N // 32, body, 0)


def weigh(w5, d, cs, inv_ref, s0):
    def body(r, size, carry):
        rows = [w5[r - 1 + i] for i in range(size + 2)]
        for i in range(size):
            u = rows[i + 1]
            dx, dy = rows[i] - rows[i + 2], roll(u, 1) - roll(u, -1)
            xp, yp = jnp.maximum(dx, 0.0), jnp.maximum(dy, 0.0)
            xm, ym = xp - dx, yp - dy
            t = 4.0 + ((xp + xm) + (yp + ym))
            inv = recip(t)
            inv_ref[r + i] = inv
            s0[r + i] = d[r + i] * t
            for n, p in enumerate((xp, xm, yp, ym)):
                cs[r + i, n] = inv + p * inv
        return carry

    row_loop(PAD + 5, ROWS - 2 * (PAD + 5), body, block=WEIGH)


def fp(src, dst, cs, margin, inv_ref=None):
    def body(r, size, total):
        rows = [src[r - 1 + i] for i in range(size + 2)]
        for i in range(size):
            u = rows[i + 1]
            along_x = cs[r + i - 1, 0] * rows[i] + cs[r + i + 1, 1] * rows[i + 2]
            along_y = roll(cs[r + i, 2] * u, 1) + roll(cs[r + i, 3] * u, -1)
            fresh = along_x + along_y
            if inv_ref is not None:
                fresh = fresh * inv_ref[r + i]
                total = total + fresh
            dst[r + i] = fresh
        return total

    return row_loop(PAD + margin, ROWS - 2 * (PAD + margin), body, jnp.zeros((SUB, 128), F32), block=FP)


def last_sums_kernel(
    sx, d_hbm, w3_hbm, d_halo, y0, y1, row1, row2, value_hbm, density, sums, lam4_row,
    w3, v4, w5, cs, dx, da, db, inv, scratch, value, w3_sems, d_sem, value_sem,
):
    size = WAVE
    first = PAD + 2
    copies = [pltpu.make_async_copy(w3_hbm.at[pl.ds(0, first + 1)], w3.at[pl.ds(0, first + 1)], w3_sems.at[5])]

    def wave(i):
        part = pl.ds(first + 1 + i * size, size)
        return pltpu.make_async_copy(w3_hbm.at[part], w3.at[part], w3_sems.at[i])

    head = copies[0]
    head.start()
    for i in range(5):
        wave(i).start()
    used = pl.ds(ROW0, N)
    load_d = pltpu.make_async_copy(d_hbm.at[used], dx.at[used], d_sem)
    load_d.start()
    _, lam2, _ = first_means(row1[...])
    lam3, lam4, mean4 = second_means(row2[...], lam2)
    lam4_row[...] = to_row([lam4])
    head.wait()
    sweep(w3, sx, v4, spread(8.0 * lam3), spread(mean4), 3, before=lambda i: wave(i).wait())
    total5 = sweep(v4, sx, w5, spread(8.0 * lam4), None, 4, True)
    transpose_out(w5, scratch, value)
    store = pltpu.make_async_copy(value, value_hbm, value_sem)
    store.start()
    load_d.wait()
    _, odd_y = odd()
    masks = halo_masks()
    for i, at in halo_rows():
        if HALO - D_HALO <= i < HALO + D_HALO:
            fl, fr = pick(odd_y, y0[i // 4], y1[i // 4]), pick(odd_y, y1[i // 4], y0[i // 4])
            d = d_halo[i - (HALO - D_HALO)]
            dx[at, 0:K] = d[:K]
            dx[at, K:SUB] = beyond(d[K:], fl, fr, i % 4, masks, True)
    weigh(w5, dx, cs, inv, db)
    src, other = db, da
    for n in range(5):
        mass = fp(src, other, cs, 6 + n, inv if n == 4 else None)
        src, other = other, src
    sums[...] = to_row([own(total5, 4), own(mass, 10)])
    transpose_out(src, scratch, density)
    store.wait()


def finish_kernel(
    value_hbm, density_in, lam4_row, row3, value_out, density_out, ergodic_out, value_in, value, density, ergodic, sems, e_sem
):
    part = lambda i: pl.ds(4 * i, 4)
    loads = [pltpu.make_async_copy(value_hbm.at[part(i)], value_in.at[part(i)], sems.at[0, i]) for i in range(4)]
    for load in loads:
        load.start()
    shift = from_row(row3[...], 0) * (1.0 / CELLS)
    scale = CELLS / from_row(row3[...], 1)
    ergodic[...] = (lam4_row[...] + row3[...] * (2.0 / CELLS))[0, :K]
    stores = [pltpu.make_async_copy(ergodic, ergodic_out, e_sem)]
    stores[0].start()
    for i in range(4):
        for k in range(4 * i, 4 * i + 4):
            density[k] = density_in[k] * scale[k : k + 1]
        stores.append(pltpu.make_async_copy(density.at[part(i)], density_out.at[part(i)], sems.at[1, i]))
        stores[-1].start()
    for i in range(4):
        loads[i].wait()
        for k in range(4 * i, 4 * i + 4):
            value[k] = value_in[k] - shift[k : k + 1]
        stores.append(pltpu.make_async_copy(value.at[part(i)], value_out.at[part(i)], sems.at[2, i]))
        stores[-1].start()
    for store in stores:
        store.wait()


VMEM = pl.BlockSpec(memory_space=pltpu.VMEM)
HBM = pl.BlockSpec(memory_space=pltpu.HBM)
DMA = pltpu.SemaphoreType.DMA


def kernel(body, outs, ins, scratch=(), aliases=None, vmem=16):
    call = pl.pallas_call(
        body,
        out_shape=[
            pltpu.HBM(shape[0], F32) if isinstance(shape, list) else jax.ShapeDtypeStruct(shape, F32) for shape in outs
        ],
        in_specs=ins,
        out_specs=[HBM if isinstance(shape, list) else VMEM for shape in outs],
        scratch_shapes=[pltpu.VMEM(shape, F32) if isinstance(shape, tuple) else shape for shape in scratch],
        input_output_aliases=aliases or {},
        compiler_params=pltpu.CompilerParams(vmem_limit_bytes=vmem * 1024 * 1024),
    )

    def run(*operands):
        return call(*[pltpu.with_memory_space_constraint(x, pltpu.HBM) if spec is HBM else x for x, spec in zip(operands, ins)])

    return run


def exchange(first, second, axes):
    pairs = [(i, i ^ 1) for i in range(16)], [(i, (i + 1 if i % 2 else i - 1) % 16) for i in range(16)]
    return lax.ppermute(first, axes, pairs[0]), lax.ppermute(second, axes, pairs[1])


def total_over_devices(row):
    rows = jnp.broadcast_to(row[None], (DEVICES, 1, 128))
    return jnp.sum(lax.all_to_all(rows, AXES, 0, 0), axis=0)


def shards(cost, density_start, coupling):
    big = (ROWS, SUB, 128)
    row = (1, 128)
    strip = (HALO + D_HALO, K, 128)
    block = (K, N, N)
    sx, dx, x0, x1, y0, y1 = kernel(
        source_kernel,
        [big, big, strip, strip, (32, 8, 128), (32, 8, 128)],
        [HBM, HBM, HBM],
        scratch=[pltpu.SMEM((K, K), F32), block, block, DMA((2, N // CHUNK)), DMA],
    )(coupling, cost, density_start)
    y0, y1 = exchange(y0, y1, GY)
    x0, x1 = exchange(x0, x1, GX)
    sx, d_hbm, sums = kernel(
        windows_kernel, [big, [big], (3, SUB, 128)], [VMEM] * 4, scratch=[big, DMA], aliases={0: 0}
    )(sx, dx, y0, y1)
    sx, d_halo, y0, y1, sums = kernel(
        first_sums_kernel, [big, (2 * D_HALO, SUB, 128), (5, 8, 128), (5, 8, 128), row], [VMEM] * 4, aliases={0: 0}
    )(sx, sums, x0, x1)
    y0, y1 = exchange(y0, y1, GY)
    row1 = total_over_devices(sums)
    sx, w3, sums = kernel(
        second_sums_kernel, [big, [big], row], [VMEM] * 4, scratch=[big, big, DMA], aliases={0: 0}
    )(sx, y0, y1, row1)
    row2 = total_over_devices(sums)
    value, density, sums, lam4 = kernel(
        last_sums_kernel,
        [[block], block, row, row],
        [VMEM, HBM, HBM] + [VMEM] * 5,
        scratch=[big, big, big, (ROWS, 4, SUB, 128), big, big, big, big, (64, K, 128), block, DMA((6,)), DMA, DMA],
        vmem=28,
    )(sx, d_hbm, w3, d_halo, y0, y1, row1, row2)
    row3 = total_over_devices(sums)
    value, density, ergodic = kernel(
        finish_kernel,
        [[block], [block], [(K,)]],
        [HBM] + [VMEM] * 3,
        scratch=[block, block, block, (K,), DMA((3, 4)), DMA],
    )(value, density, lam4, row3)
    return value, density, ergodic


def solution(mesh):
    torus = Mesh(mesh.devices.reshape(4, 2, 2, 2, 8), AXES)
    specs = (P(None, GX, GY), P(None, GX, GY), P())
    return jax.shard_map(shards, mesh=torus, in_specs=specs, out_specs=specs, check_vma=False)
```

```python
import functools

import jax
import jax.numpy as jnp
from jax import lax
from jax.experimental import pallas as pl
from jax.experimental.pallas import tpu as pltpu
from jax.sharding import Mesh
from jax.sharding import PartitionSpec as P

HALO = 10
D_HALO = 5
PAD = 4
ROW0 = PAD + HALO
N = 128
ROWS = N + 2 * ROW0
K = 16
SUB = 24
AXES = ("y", "xh", "c", "xl", "z")
GX = ("y", "xh", "c")
GY = ("xl", "z")
DEVICES = 256
CELLS = 2048.0 * 2048.0
SLOT = (0, 16, 64, 80)
BLOCK = 75
WEIGH = 72
FP = 140
SUMS = 64
GROUPS = 32
CHUNK = 64
WAVE = 29
F32 = jnp.float32


def lanes(shape):
    return lax.broadcasted_iota(jnp.int32, shape, 1)


def roll(x, shift):
    return pltpu.roll(x, shift % 128, 1)


def between(lane, low, high):
    return (lane >= low) & (lane < high)


def recip(x):
    return 1.0 / x


def odd():
    return lax.axis_index("c") == 1, lax.axis_index("z") % 2 == 1


def pick(flag, yes, no):
    return jnp.where(jnp.broadcast_to(flag, yes.shape), yes, no)


def pack(rows, left):
    lane = lanes((8, 128))
    out = jnp.zeros((8, 128), F32)
    for (s0, s1, d0, d1), base in zip(rows, SLOT):
        for half, (s, d) in enumerate(((s0, d0), (s1, d1))):
            at = base + 32 * half
            ds = roll(s, at if left else at + HALO)
            dd = roll(d, at + HALO if left else at + HALO + D_HALO)
            out = jnp.where(between(lane, at, at + HALO), ds, out)
            out = jnp.where(between(lane, at + HALO, at + HALO + D_HALO), dd, out)
    return out


def windows(a, b):
    lane = lanes((8, 128))
    left = jnp.where(lane < 32, roll(a, 10), roll(b, 42))
    right = jnp.where(lane < 96, roll(a, 86), roll(b, 118))
    return jnp.where(lane < 64, left, right)


def halo_masks():
    lane = lanes((8, 128))
    left = between(lane, 0, 10) | between(lane, 32, 42)
    right = between(lane, 86, 96) | between(lane, 118, 128)
    return left, right


def beyond(window, from_left, from_right, i, masks, density):
    base = SLOT[i]
    a = roll(from_left, -base - 5 if density else -base)
    b = roll(from_right, 76 - base if density else 86 - base)
    return jnp.where(masks[0], a, jnp.where(masks[1], b, window))


def own(total, margin):
    lane = lanes((K, 128))
    main = jnp.where(between(lane, margin, N - margin), total[:K], 0.0)
    main = jnp.sum(main, axis=1, keepdims=True)
    if margin == 0:
        return main
    edge = total[K:]
    lane = lanes((8, 128))
    halves = []
    for half in range(2):
        at = 32 * half
        mask = between(lane, at + 10, at + 10 + margin) | between(lane, 64 + at + 22 - margin, 64 + at + 22)
        halves.append(jnp.sum(jnp.where(mask, edge, 0.0), axis=1, keepdims=True))
    return main + jnp.concatenate(halves, axis=0)


def to_row(columns):
    lane, cls = lanes((K, 128)), lax.broadcasted_iota(jnp.int32, (K, 128), 0)
    grid = jnp.zeros((K, 128), F32)
    for i, column in enumerate(columns):
        grid = jnp.where(lane == cls + K * i, column, grid)
    return jnp.sum(grid, axis=0, keepdims=True)


def from_row(row, i):
    lane, cls = lanes((K, 128)), lax.broadcasted_iota(jnp.int32, (K, 128), 0)
    return jnp.sum(jnp.where(lane == cls + K * i, row, 0.0), axis=1, keepdims=True)


def spread(column):
    wide = jnp.broadcast_to(column, (K, 128))
    lane = lanes((8, 128))
    edge = jnp.where((lane // 32) % 2 == 0, wide[:8], wide[8:])
    return jnp.concatenate([wide, edge], axis=0)


def parts(up, mid, down, s):
    left, right = roll(mid, 1), roll(mid, -1)
    px = 2.0 + jnp.abs(up - down)
    py = 2.0 + jnp.abs(left - right)
    n = s + (px * (2.0 * (up + down) + (4.0 - px)) + py * (2.0 * (left + right) + (4.0 - py)))
    return n, recip(px + py)


def row_loop(first, count, body, init=0, before=None, block=None):
    blocks = -(-count // (block or BLOCK))
    size = -(-count // blocks)
    first = first - (blocks * size - count) // 2

    def step(i, carry):
        if before is not None:
            before(i)
        return body(first + i * size, size, carry)

    return lax.fori_loop(0, blocks, step, init)


def sweep(src, s_ref, dst, lam8, minus, margin, summed=False, before=None, half=False):
    def body(r, size, total):
        rows = [src[r - 1 + i] for i in range(size + 2)]
        if half:
            rows = [row * 0.0625 + 0.5 for row in rows]
        for i in range(size):
            n, inv = parts(rows[i], rows[i + 1], rows[i + 2], s_ref[r + i] - lam8)
            w = n * (0.25 * inv)
            if minus is not None:
                w = w - minus
            dst[r + i] = w
        return total

    row_loop(PAD + margin, ROWS - 2 * (PAD + margin), body, before=before, block=32 if before else None)
    if summed:
        def add(r, size, total):
            for i in range(size):
                total = total + dst[r + i]
            return total

        return row_loop(ROW0, N, add, jnp.zeros((SUB, 128), F32), block=SUMS)


def sweep_sums(src, s_ref, half, first=ROW0, count=N):
    def body(r, size, carry):
        a, b = carry
        rows = [src[r - 1 + i] for i in range(size + 2)]
        if half:
            rows = [row * 0.0625 + 0.5 for row in rows]
        for i in range(size):
            n, inv = parts(rows[i], rows[i + 1], rows[i + 2], s_ref[r + i])
            a = a + n * inv
            b = b + inv
        return a, b

    zero = jnp.zeros((SUB, 128), F32)
    return row_loop(first, count, body, (zero, zero), block=count // 2)


def source_kernel(c_hbm, cost_hbm, d_hbm, sx, dx, x0, x1, y0, y1, c_ref, cost_ref, d_ref, sems, c_sem):
    odd_x, odd_y = odd()
    s2, d2 = sx.reshape(ROWS * SUB, 128), dx.reshape(ROWS * SUB, 128)
    coupling = pltpu.make_async_copy(c_hbm, c_ref, c_sem)
    coupling.start()

    def copies(i):
        part = pl.ds(pl.multiple_of(i * CHUNK, CHUNK), CHUNK)
        return (
            pltpu.make_async_copy(d_hbm.at[:, part], d_ref.at[:, part], sems.at[0, i]),
            pltpu.make_async_copy(cost_hbm.at[:, part], cost_ref.at[:, part], sems.at[1, i]),
        )

    for i in range(N // CHUNK):
        for copy in copies(i):
            copy.start()
    coupling.wait()

    def chunk(i, carry):
        for copy in copies(i):
            copy.wait()
        for part in range(CHUNK // 8):
            r = pl.multiple_of(i * CHUNK + part * 8, 8)
            dens = [d_ref[j, pl.ds(r, 8), :] for j in range(K)]
            base = (ROW0 + r) * SUB
            for j in range(K):
                d2[pl.ds(base + j, 8, stride=SUB), :] = dens[j]
            for k in range(K):
                acc = cost_ref[k, pl.ds(r, 8), :]
                for j in range(K):
                    acc = acc + c_ref[k, j] * dens[j]
                s2[pl.ds(base + k, 8, stride=SUB), :] = acc * 8.0 - 8.0
        for g in range(CHUNK // 4):
            g = i * (CHUNK // 4) + g
            r = ROW0 + g * 4
            rows = [(sx[r + i, 0:8], sx[r + i, 8:16], dx[r + i, 0:8], dx[r + i, 8:16]) for i in range(4)]
            left, right = pack(rows, True), pack(rows, False)
            y0[g] = pick(odd_y, left, right)
            y1[g] = pick(odd_y, right, left)
        return carry

    lax.fori_loop(0, N // CHUNK, chunk, 0)

    tops = [sx[ROW0 + i, 0:K] for i in range(HALO)] + [dx[ROW0 + i, 0:K] for i in range(D_HALO)]
    last = ROW0 + N
    bottoms = [sx[last - HALO + i, 0:K] for i in range(HALO)] + [dx[last - D_HALO + i, 0:K] for i in range(D_HALO)]
    for i, (top, bottom) in enumerate(zip(tops, bottoms)):
        x0[i] = pick(odd_x, top, bottom)
        x1[i] = pick(odd_x, bottom, top)


def halo_rows():
    return [(i, PAD + i) for i in range(HALO)] + [(HALO + i, ROW0 + N + i) for i in range(HALO)]


def windows_kernel(s_in, d_in, y0, y1, sx, d_hbm, sums, dx, d_sem):
    del s_in
    _, odd_y = odd()
    masks = halo_masks()

    def d_group(g0, carry):
        for g in range(GROUPS):
            g = g0 * GROUPS + g
            fl, fr = pick(odd_y, y0[g], y1[g]), pick(odd_y, y1[g], y0[g])
            for i in range(4):
                r = ROW0 + g * 4 + i
                d = d_in[r, 0:K]
                dx[r, 0:K] = d
                dx[r, K:SUB] = beyond(windows(d[:8], d[8:]), fl, fr, i, masks, True)
        return carry

    lax.fori_loop(0, N // 4 // GROUPS, d_group, 0)
    used = pl.ds(ROW0, N)
    store_d = pltpu.make_async_copy(dx.at[used], d_hbm.at[used], d_sem)
    store_d.start()

    def group(g0, total):
        for g in range(GROUPS):
            g = g0 * GROUPS + g
            fl, fr = pick(odd_y, y0[g], y1[g]), pick(odd_y, y1[g], y0[g])
            for i in range(4):
                r = ROW0 + g * 4 + i
                s = sx[r, 0:K]
                total = total + s
                sx[r, K:SUB] = beyond(windows(s[:8], s[8:]), fl, fr, i, masks, False)
        return total

    total = lax.fori_loop(0, N // 4 // GROUPS, group, jnp.zeros((K, 128), F32))
    a, b = sweep_sums(sx, sx, True, ROW0 + 1, N - 2)
    sums[0, 0:K] = total
    sums[1] = a
    sums[2] = b
    store_d.wait()


def first_sums_kernel(s_in, sums_in, x0, x1, sx, d_halo, y0, y1, sums):
    del s_in
    odd_x, odd_y = odd()
    zero = jnp.zeros((8, 128), F32)
    packed = []
    for i, at in halo_rows():
        above, below = (x0, x1), (x1, x0)
        yes, no = above if i < HALO else below
        s = pick(odd_x, yes[i % HALO], no[i % HALO])
        sx[at, 0:K] = s
        sx[at, K:SUB] = windows(s[:8], s[8:])
        if HALO - D_HALO <= i < HALO + D_HALO:
            j = HALO + i % D_HALO
            d = pick(odd_x, yes[j], no[j])
            d_halo[i - (HALO - D_HALO), 0:K] = d
            d_halo[i - (HALO - D_HALO), K:SUB] = windows(d[:8], d[8:])
            packed.append((s[:8], s[8:], d[:8], d[8:]))
        else:
            packed.append((s[:8], s[8:], zero, zero))
    for g in range(5):
        rows = packed[4 * g : 4 * g + 4]
        left, right = pack(rows, True), pack(rows, False)
        y0[g] = pick(odd_y, left, right)
        y1[g] = pick(odd_y, right, left)
    a, b = sums_in[1], sums_in[2]
    for r in (ROW0, ROW0 + N - 1):
        up, mid, down = [sx[r + i] * 0.0625 + 0.5 for i in (-1, 0, 1)]
        n, inv = parts(up, mid, down, sx[r])
        a = a + n * inv
        b = b + inv
    sums[...] = to_row([jnp.sum(sums_in[0, 0:K], axis=1, keepdims=True), own(a, 1), own(b, 1)])


def first_means(row):
    lam1 = from_row(row, 0) * (0.125 / CELLS) + 1.0
    mean2 = from_row(row, 1) * (0.25 / CELLS) - lam1 * (from_row(row, 2) * (2.0 / CELLS))
    return lam1, 2.0 * mean2, mean2


def second_means(row, lam2):
    lam3 = lam2 + from_row(row, 0) * (2.0 / CELLS)
    mean4 = from_row(row, 1) * (0.25 / CELLS) - lam3 * (from_row(row, 2) * (2.0 / CELLS))
    return lam3, lam2 + 2.0 * mean4, mean4


def second_sums_kernel(s_in, y0, y1, row1, sx, w3_hbm, sums, v2, w3, sem):
    del s_in
    _, odd_y = odd()
    masks = halo_masks()
    for i, at in halo_rows():
        fl, fr = pick(odd_y, y0[i // 4], y1[i // 4]), pick(odd_y, y1[i // 4], y0[i // 4])
        sx[at, K:SUB] = beyond(sx[at, K:SUB], fl, fr, i % 4, masks, False)

    lam1, lam2, mean2 = first_means(row1[...])
    sweep(sx, sx, v2, spread(8.0 * lam1), spread(mean2), 1, half=True)
    total = sweep(v2, sx, w3, spread(8.0 * lam2), None, 2, True)
    store = pltpu.make_async_copy(w3, w3_hbm, sem)
    store.start()
    a, b = sweep_sums(w3, sx, False)
    sums[...] = to_row([own(total, 2), own(a, 3), own(b, 3)])
    store.wait()


def transpose_out(src, scratch, out):
    lane = lanes((8, 128))
    low, high = lane < 10, lane >= 118
    flat = scratch.reshape(2 * 32 * K, 128)

    def body(g, carry):
        slot = 0
        for i in range(64):
            r = g * 64 + i
            e = src[ROW0 + r, K:SUB]
            for half in range(2):
                a = src[ROW0 + r, 8 * half : 8 * half + 8]
                left = roll(e, -10 - 32 * half)
                right = roll(e, 42 - 32 * half)
                scratch[slot + i, 8 * half : 8 * half + 8] = jnp.where(low, left, jnp.where(high, right, a))
            if i % 8 == 7:
                at = pl.multiple_of(g * 64 + i - 7, 8)
                for k in range(K):
                    out[k, pl.ds(at, 8), :] = flat[pl.ds((slot + i - 7) * K + k, 8, stride=K), :]
        return carry

    lax.fori_loop(0, N // 64, body, 0)


def weigh(w5, d, cs, inv_ref, s0):
    def body(r, size, carry):
        rows = [w5[r - 1 + i] for i in range(size + 2)]
        for i in range(size):
            u = rows[i + 1]
            dx, dy = rows[i] - rows[i + 2], roll(u, 1) - roll(u, -1)
            xp, yp = jnp.maximum(dx, 0.0), jnp.maximum(dy, 0.0)
            xm, ym = xp - dx, yp - dy
            t = 4.0 + ((xp + xm) + (yp + ym))
            inv = recip(t)
            inv_ref[r + i] = inv
            s0[r + i] = d[r + i] * t
            for n, p in enumerate((xp, xm, yp, ym)):
                cs[r + i, n] = inv + p * inv
        return carry

    row_loop(PAD + 5, ROWS - 2 * (PAD + 5), body, block=WEIGH)


def fp(src, dst, cs, margin, inv_ref=None):
    def body(r, size, total):
        rows = [src[r - 1 + i] for i in range(size + 2)]
        for i in range(size):
            u = rows[i + 1]
            along_x = cs[r + i - 1, 0] * rows[i] + cs[r + i + 1, 1] * rows[i + 2]
            along_y = roll(cs[r + i, 2] * u, 1) + roll(cs[r + i, 3] * u, -1)
            fresh = along_x + along_y
            if inv_ref is not None:
                fresh = fresh * inv_ref[r + i]
                total = total + fresh
            dst[r + i] = fresh
        return total

    return row_loop(PAD + margin, ROWS - 2 * (PAD + margin), body, jnp.zeros((SUB, 128), F32), block=FP)


def last_sums_kernel(
    sx, d_hbm, w3_hbm, d_halo, y0, y1, row1, row2, value_hbm, density, sums, lam4_row,
    w3, v4, w5, cs, dx, da, db, inv, scratch, value, w3_sems, d_sem, value_sem,
):
    size = WAVE
    first = PAD + 2
    copies = [pltpu.make_async_copy(w3_hbm.at[pl.ds(0, first + 1)], w3.at[pl.ds(0, first + 1)], w3_sems.at[5])]

    def wave(i):
        part = pl.ds(first + 1 + i * size, size)
        return pltpu.make_async_copy(w3_hbm.at[part], w3.at[part], w3_sems.at[i])

    head = copies[0]
    head.start()
    for i in range(5):
        wave(i).start()
    used = pl.ds(ROW0, N)
    load_d = pltpu.make_async_copy(d_hbm.at[used], dx.at[used], d_sem)
    load_d.start()
    _, lam2, _ = first_means(row1[...])
    lam3, lam4, mean4 = second_means(row2[...], lam2)
    lam4_row[...] = to_row([lam4])
    head.wait()
    sweep(w3, sx, v4, spread(8.0 * lam3), spread(mean4), 3, before=lambda i: wave(i).wait())
    total5 = sweep(v4, sx, w5, spread(8.0 * lam4), None, 4, True)
    transpose_out(w5, scratch, value)
    store = pltpu.make_async_copy(value, value_hbm, value_sem)
    store.start()
    load_d.wait()
    _, odd_y = odd()
    masks = halo_masks()
    for i, at in halo_rows():
        if HALO - D_HALO <= i < HALO + D_HALO:
            fl, fr = pick(odd_y, y0[i // 4], y1[i // 4]), pick(odd_y, y1[i // 4], y0[i // 4])
            d = d_halo[i - (HALO - D_HALO)]
            dx[at, 0:K] = d[:K]
            dx[at, K:SUB] = beyond(d[K:], fl, fr, i % 4, masks, True)
    weigh(w5, dx, cs, inv, db)
    src, other = db, da
    for n in range(5):
        mass = fp(src, other, cs, 6 + n, inv if n == 4 else None)
        src, other = other, src
    sums[...] = to_row([own(total5, 4), own(mass, 10)])
    transpose_out(src, scratch, density)
    store.wait()


def finish_kernel(
    value_hbm, density_in, lam4_row, row3, value_out, density_out, ergodic_out, value_in, value, density, ergodic, sems, e_sem
):
    part = lambda i: pl.ds(4 * i, 4)
    loads = [pltpu.make_async_copy(value_hbm.at[part(i)], value_in.at[part(i)], sems.at[0, i]) for i in range(4)]
    for load in loads:
        load.start()
    shift = from_row(row3[...], 0) * (1.0 / CELLS)
    scale = CELLS / from_row(row3[...], 1)
    ergodic[...] = (lam4_row[...] + row3[...] * (2.0 / CELLS))[0, :K]
    stores = [pltpu.make_async_copy(ergodic, ergodic_out, e_sem)]
    stores[0].start()
    for i in range(4):
        for k in range(4 * i, 4 * i + 4):
            density[k] = density_in[k] * scale[k : k + 1]
        stores.append(pltpu.make_async_copy(density.at[part(i)], density_out.at[part(i)], sems.at[1, i]))
        stores[-1].start()
    for i in range(4):
        loads[i].wait()
        for k in range(4 * i, 4 * i + 4):
            value[k] = value_in[k] - shift[k : k + 1]
        stores.append(pltpu.make_async_copy(value.at[part(i)], value_out.at[part(i)], sems.at[2, i]))
        stores[-1].start()
    for store in stores:
        store.wait()


VMEM = pl.BlockSpec(memory_space=pltpu.VMEM)
HBM = pl.BlockSpec(memory_space=pltpu.HBM)
DMA = pltpu.SemaphoreType.DMA


def kernel(body, outs, ins, scratch=(), aliases=None, vmem=16):
    call = pl.pallas_call(
        body,
        out_shape=[
            pltpu.HBM(shape[0], F32) if isinstance(shape, list) else jax.ShapeDtypeStruct(shape, F32) for shape in outs
        ],
        in_specs=ins,
        out_specs=[HBM if isinstance(shape, list) else VMEM for shape in outs],
        scratch_shapes=[pltpu.VMEM(shape, F32) if isinstance(shape, tuple) else shape for shape in scratch],
        input_output_aliases=aliases or {},
        compiler_params=pltpu.CompilerParams(vmem_limit_bytes=vmem * 1024 * 1024),
    )

    def run(*operands):
        return call(*[pltpu.with_memory_space_constraint(x, pltpu.HBM) if spec is HBM else x for x, spec in zip(operands, ins)])

    return run


def exchange(first, second, axes):
    pairs = [(i, i ^ 1) for i in range(16)], [(i, (i + 1 if i % 2 else i - 1) % 16) for i in range(16)]
    return lax.ppermute(first, axes, pairs[0]), lax.ppermute(second, axes, pairs[1])


def total_over_devices(row):
    rows = jnp.broadcast_to(row[None], (DEVICES, 1, 128))
    return jnp.sum(lax.all_to_all(rows, AXES, 0, 0), axis=0)


def shards(cost, density_start, coupling):
    big = (ROWS, SUB, 128)
    row = (1, 128)
    strip = (HALO + D_HALO, K, 128)
    block = (K, N, N)
    sx, dx, x0, x1, y0, y1 = kernel(
        source_kernel,
        [big, big, strip, strip, (32, 8, 128), (32, 8, 128)],
        [HBM, HBM, HBM],
        scratch=[pltpu.SMEM((K, K), F32), block, block, DMA((2, N // CHUNK)), DMA],
    )(coupling, cost, density_start)
    y0, y1 = exchange(y0, y1, GY)
    x0, x1 = exchange(x0, x1, GX)
    sx, d_hbm, sums = kernel(
        windows_kernel, [big, [big], (3, SUB, 128)], [VMEM] * 4, scratch=[big, DMA], aliases={0: 0}
    )(sx, dx, y0, y1)
    sx, d_halo, y0, y1, sums = kernel(
        first_sums_kernel, [big, (2 * D_HALO, SUB, 128), (5, 8, 128), (5, 8, 128), row], [VMEM] * 4, aliases={0: 0}
    )(sx, sums, x0, x1)
    y0, y1 = exchange(y0, y1, GY)
    row1 = total_over_devices(sums)
    sx, w3, sums = kernel(
        second_sums_kernel, [big, [big], row], [VMEM] * 4, scratch=[big, big, DMA], aliases={0: 0}
    )(sx, y0, y1, row1)
    row2 = total_over_devices(sums)
    value, density, sums, lam4 = kernel(
        last_sums_kernel,
        [[block], block, row, row],
        [VMEM, HBM, HBM] + [VMEM] * 5,
        scratch=[big, big, big, (ROWS, 4, SUB, 128), big, big, big, big, (64, K, 128), block, DMA((6,)), DMA, DMA],
        vmem=28,
    )(sx, d_hbm, w3, d_halo, y0, y1, row1, row2)
    row3 = total_over_devices(sums)
    value, density, ergodic = kernel(
        finish_kernel,
        [[block], [block], [(K,)]],
        [HBM] + [VMEM] * 3,
        scratch=[block, block, block, (K,), DMA((3, 4)), DMA],
    )(value, density, lam4, row3)
    return value, density, ergodic


def solution(mesh):
    torus = Mesh(mesh.devices.reshape(4, 2, 2, 2, 8), AXES)
    specs = (P(None, GX, GY), P(None, GX, GY), P())
    return jax.shard_map(shards, mesh=torus, in_specs=specs, out_specs=specs, check_vma=False)
```
